128 devices in a mesh: seq: 16 (over y, x), dp: 4 (over z), tensor: 2 (over core).
Axes of the slice: x: 4, y: 4, z: 4, core: 2. Of those that a mesh axis runs over, the one named last changes fastest.
Arguments:
- q_proj: bfloat16 [2048, 8, 4096], P('seq', 'dp', 'tensor'), may hold values from -122 to 122
- k_proj: bfloat16 [2048, 8, 1024], P('seq', 'dp', 'tensor'), may hold values from -6.1 to 6.1
- v_proj: bfloat16 [2048, 8, 1024], P('seq', 'dp', 'tensor'), may hold values from -6 to 6
- lm_cotangent: bfloat16 [2048, 8, 4096], P('seq', 'dp', 'tensor'), may hold values from -1.5 to 1.5
- query_emb: bfloat16 [256, 4096], P('dp', 'tensor'), may hold values from -320 to 320
- doc_lengths: int32 [8], P('dp'), may hold values from 512 to 2048, as said below
- positive_ids: int32 [256], P('dp'), may hold values from 0 to 7
- hard_ids: int32 [256, 4], P('dp'), may hold values from 0 to 7
Outputs:
- grad_q: bfloat16 [2048, 8, 4096], P('seq', 'dp', 'tensor')
- grad_k: bfloat16 [2048, 8, 1024], P('seq', 'dp', 'tensor')
- grad_v: bfloat16 [2048, 8, 1024], P('seq', 'dp', 'tensor')
- query_grad: float32 [256, 4096], P('dp', 'tensor')
- loss: float32 [], replicated
The draws below stay inside these ranges and needn't reach their ends.
Inputs may be any that keep to these rules, and one draw needn't show every extreme that they name: `doc_lengths`: every document has at least one token; some document fills all 2048 positions.
All inputs are finite; a program needn't handle non-finite values.
Results may differ from the reference program's by a relative error of at most 0.034.
Values may be sent and summed in bfloat16 or wider, within the bound.
A program may use at most 128 MiB of HBM per device.

```python
import jax
import jax.numpy as jnp
from jax import lax

D = 4096
QH = 32
KVH = 8
HD = 128
LEN = 2048
K_NEG = 4
DOCS = 8
QRY = 256


def base_keys(key):
    return jnp.clip(jax.random.normal(key, (LEN, DOCS, KVH, HD), jnp.float32), -6.0, 6.0)


def draw_k_proj(key, part):
    shared = base_keys(key)
    return shared.reshape(LEN, DOCS, KVH * HD).astype(jnp.bfloat16)


def draw_q_proj(key, part):
    key = jax.random.fold_in(key, 7)
    fresh = jnp.clip(jax.random.normal(key, (LEN, DOCS, QH, HD), jnp.float32), -6.0, 6.0)
    return fresh.reshape(LEN, DOCS, QH * HD).astype(jnp.bfloat16)


def scaled_rows(key, values, top):
    row_key = jax.random.fold_in(key, 11)
    rows = jnp.exp(jax.random.uniform(row_key, (QRY, 1), jnp.float32, 0.0, 2.302585))
    columns = jnp.exp(jnp.linspace(0.0, top, D, dtype=jnp.float32))[None, :]
    return values * rows * columns


def draw_query_emb(key, part):
    key = jax.random.fold_in(key, 9)
    values = jnp.clip(jax.random.normal(key, (QRY, D), jnp.float32), -4.0, 4.0)
    out = scaled_rows(key, values, 1.3862944)
    return out.astype(jnp.bfloat16)


def draw_doc_lengths(key, part):
    key = jax.random.fold_in(key, 5)
    key_lengths, key_chosen = jax.random.split(key)
    drawn = jax.random.randint(key_lengths, (DOCS,), LEN // 4, LEN + 1)
    chosen = jax.random.randint(key_chosen, (), 0, DOCS)
    return jnp.where(jnp.arange(DOCS) == chosen, LEN, drawn).astype(jnp.int32)


def set_ends(entries, rng, smallest, largest):
    place = [jax.random.randint(jax.random.fold_in(rng, axis), (), 0, length) for axis, length in enumerate(entries.shape)]
    longest = entries.shape.index(max(entries.shape))
    neighbour = place[:longest] + [(place[longest] + 1) % entries.shape[longest]] + place[longest + 1:]
    return entries.at[tuple(place)].set(smallest).at[tuple(neighbour)].set(largest)


def block_levels(rng, shape, shards, least, high):
    factor_of = 1.0
    for position, shards_of in shards:
        steps = jax.random.uniform(jax.random.fold_in(jax.random.fold_in(rng, 6), position), (shards_of,), jnp.float32, least / len(shards), high / len(shards))
        factor_of = factor_of * jnp.repeat(jnp.exp(steps), shape[position] // shards_of).reshape((-1,) + (1,) * (len(shape) - 1 - position))
    return factor_of


def scatter_about(own_key, dims, scale, most, pieces=(), kind=jnp.bfloat16):
    result = jax.random.normal(own_key, dims, jnp.float32) * scale
    if len(pieces) > 0:
        result = block_levels(own_key, dims, pieces, -0.22, 0.18) * result
    return jnp.clip(result, min=-most, max=most).astype(kind)


def setup_inputs(seed: int = 0) -> dict:
    streams_of = jax.random.split(jax.random.key(seed), 9)
    q_proj = draw_q_proj(jax.random.fold_in(streams_of[8], 71), 0)
    k_proj = draw_k_proj(jax.random.fold_in(streams_of[8], 71), 0)
    v_proj = scatter_about(streams_of[2], (LEN, DOCS, KVH * HD), 1.0, 6.0, ((0, 16), (1, 4), (2, 2)))
    lm_cotangent = scatter_about(streams_of[3], (LEN, DOCS, D), 0.25, 1.5, ((0, 16), (1, 4), (2, 2)))
    query_emb = draw_query_emb(jax.random.fold_in(streams_of[8], 71), 0)
    doc_lengths = draw_doc_lengths(jax.random.fold_in(streams_of[8], 71), 0)
    positive_ids = set_ends(jax.random.randint(streams_of[6], (QRY,), 0, DOCS), jax.random.fold_in(streams_of[6], 1), 0, DOCS - 1).astype(jnp.int32)
    hard_ids = set_ends(jax.random.randint(streams_of[7], (QRY, K_NEG), 0, DOCS), jax.random.fold_in(streams_of[7], 1), 0, DOCS - 1).astype(jnp.int32)
    return {"q_proj": q_proj, "k_proj": k_proj, "v_proj": v_proj, "lm_cotangent": lm_cotangent, "query_emb": query_emb, "doc_lengths": doc_lengths, "positive_ids": positive_ids, "hard_ids": hard_ids}


NEG_BIG = -1e+30
TAU = 0.02
HARD_BOOST = 3.0
EPS = 1e-06

def query_items(array, group_size):
    shaped = array.reshape(LEN, DOCS, KVH, group_size, HD).transpose(1, 2, 0, 3, 4)
    return shaped.reshape(DOCS * KVH, LEN, group_size, HD)

def key_items(array):
    shaped = array.reshape(LEN, DOCS, KVH, HD).transpose(1, 2, 0, 3)
    return shaped.reshape(DOCS * KVH, LEN, HD)

def lowered(array):
    return lax.optimization_barrier(array.astype(jnp.bfloat16)).astype(jnp.float32)

def reference(q_proj, k_proj, v_proj, lm_cotangent, query_emb, doc_lengths, positive_ids, hard_ids):
    group_size = QH // KVH
    scale = HD ** (-0.5)
    places = jnp.arange(LEN, dtype=jnp.int32)
    queries = query_items(q_proj, group_size)
    keys_all = key_items(k_proj)
    values_all = key_items(v_proj)
    item_lengths = jnp.repeat(doc_lengths, KVH)

    def softmax_parts(query, keys, length):
        logits = jnp.einsum('qgd,kd->gqk', query.astype(jnp.float32), keys.astype(jnp.float32)) * scale
        mask = (places[:, None] >= places[None, :]) & (places[None, :] < length)
        logits = jnp.where(mask[None], logits, NEG_BIG)
        peak = lax.optimization_barrier(jnp.max(logits, -1, keepdims=True))
        expw = jnp.where(mask[None], jnp.exp(logits - peak), 0.0)
        total = lax.optimization_barrier(jnp.sum(expw, -1))
        return (expw, total)

    def forward_item(item):
        query, keys, values, length = item
        expw, total = softmax_parts(query, keys, length)
        mixed = jnp.einsum('gqk,kd->qgd', lowered(expw), values.astype(jnp.float32))
        return mixed / total.T[:, :, None]
    outputs = lax.map(forward_item, (queries, keys_all, values_all, item_lengths))
    out_float = outputs.reshape(DOCS, KVH, LEN, group_size, HD).transpose(2, 0, 1, 3, 4).reshape(LEN, DOCS, D)
    attn_out = out_float.astype(jnp.bfloat16)
    pooled = out_float[doc_lengths - 1, jnp.arange(DOCS)]
    doc_norm = jnp.sqrt(lax.optimization_barrier(jnp.sum(pooled * pooled, -1)) + EPS)
    doc_unit = pooled / doc_norm[:, None]
    query_float = query_emb.astype(jnp.float32)
    query_norm = jnp.sqrt(lax.optimization_barrier(jnp.sum(query_float * query_float, -1)) + EPS)
    query_unit = query_float / query_norm[:, None]
    logits = jnp.dot(query_unit, doc_unit.T, precision=lax.Precision.HIGHEST) / TAU
    doc_ids = jnp.arange(DOCS, dtype=jnp.int32)
    counts = lax.optimization_barrier(jnp.sum((hard_ids[:, :, None] == doc_ids[None, None, :]).astype(jnp.float32), 1))
    boost = 1.0 + HARD_BOOST * counts
    weighted = boost * jnp.exp(logits)
    denom = lax.optimization_barrier(jnp.sum(weighted, -1))
    target = (positive_ids[:, None] == doc_ids[None, :]).astype(jnp.float32)
    loss = jnp.mean(jnp.log(denom) - lax.optimization_barrier(jnp.sum(target * logits, -1)))
    coef = weighted / denom[:, None] - target
    query_grad = jnp.dot(coef, doc_unit, precision=lax.Precision.HIGHEST) / TAU
    doc_grad = jnp.dot(coef.T, query_unit, precision=lax.Precision.HIGHEST) / TAU
    inner = lax.optimization_barrier(jnp.sum(doc_unit * doc_grad, -1, keepdims=True))
    pooled_grad = (doc_grad - doc_unit * inner) / doc_norm[:, None]
    valid = places[:, None] < doc_lengths[None, :]
    selector = (places[:, None] == doc_lengths[None, :] - 1).astype(jnp.float32)
    cotangent = jnp.where(valid[:, :, None], lm_cotangent.astype(jnp.float32), 0.0)
    cotangent = cotangent + selector[:, :, None] * pooled_grad[None, :, :]
    d_out = cotangent.astype(jnp.bfloat16)
    d_items = query_items(d_out, group_size)
    out_items = query_items(attn_out, group_size)

    def backward_item(item):
        query, keys, values, length, grad_out, mixed = item
        expw, total = softmax_parts(query, keys, length)
        probs = expw / total[:, :, None]
        out_grad = grad_out.astype(jnp.float32)
        d_vec = lax.optimization_barrier(jnp.sum(out_grad * mixed.astype(jnp.float32), -1)).T
        grad_value = jnp.einsum('gqk,qgd->kd', lowered(probs), out_grad)
        grad_p = jnp.einsum('qgd,kd->gqk', out_grad, values.astype(jnp.float32))
        grad_s = lowered(probs * (grad_p - d_vec[:, :, None]))
        grad_query = jnp.einsum('gqk,kd->qgd', grad_s, keys.astype(jnp.float32)) * scale
        grad_key = jnp.einsum('gqk,qgd->kd', grad_s, query.astype(jnp.float32)) * scale
        return (grad_query.astype(jnp.bfloat16), grad_key.astype(jnp.bfloat16), grad_value.astype(jnp.bfloat16))
    grad_query, grad_key, grad_value = lax.map(backward_item, (queries, keys_all, values_all, item_lengths, d_items, out_items))
    grad_q = grad_query.reshape(DOCS, KVH, LEN, group_size, HD).transpose(2, 0, 1, 3, 4).reshape(LEN, DOCS, D)
    grad_k = grad_key.reshape(DOCS, KVH, LEN, HD).transpose(2, 0, 1, 3).reshape(LEN, DOCS, KVH * HD)
    grad_v = grad_value.reshape(DOCS, KVH, LEN, HD).transpose(2, 0, 1, 3).reshape(LEN, DOCS, KVH * HD)
    return (grad_q, grad_k, grad_v, query_grad, loss)
```

```python
import functools
import math

import jax
import jax.numpy as jnp
from jax import lax
from jax.experimental import pallas as pl
from jax.experimental.pallas import tpu as pltpu
from jax.sharding import PartitionSpec as P

QH = 32
KVH = 8
HD = 128
TAU = 0.02
HARD_BOOST = 3.0
EPS = 1e-06
NEG_BIG = -1e30
SEQ = 16
DP = 4
GROUP = QH // KVH
MESH = pl.DeviceIdType.MESH
NT = (((1,), (1,)), ((), ()))
NN = (((1,), (0,)), ((), ()))
F32 = jnp.float32
BF16 = jnp.bfloat16


def places():
    seq, dp, tensor = lax.axis_index("seq"), lax.axis_index("dp"), lax.axis_index("tensor")
    return seq, dp, tensor, seq // 8, lax.rem(seq // 4, 2), lax.rem(seq, 4)


def remote(src, dst, send, recv, **device):
    return pltpu.make_async_remote_copy(
        src_ref=src, dst_ref=dst, send_sem=send, recv_sem=recv, device_id=device, device_id_type=MESH
    )


def worker(tensor, j):
    return (j // 8) * 8 + tensor * 4 + lax.rem(j // 2, 4), lax.rem(j, 2)


def greet(send_to, count):
    barrier = pltpu.get_barrier_semaphore()
    send_to(lambda **device: pl.semaphore_signal(barrier, inc=1, device_id=device, device_id_type=MESH))
    pl.semaphore_wait(barrier, count)


def when_else(cond, yes, no):
    pl.when(cond)(yes)
    pl.when(jnp.logical_not(cond))(no)


def start_to_workers(src, dst_of, send, recv):
    seq, _, tensor, _, _, _ = places()

    def body(n, _):
        head = lax.rem(seq + 2 + n // 2, 4)
        doc = lax.rem(seq // 8 + 1 + n // 8, 2)
        j = doc * 8 + head * 2 + lax.rem(n, 2)
        peer, core = worker(tensor, j)
        when_else(
            (peer == seq) & (core == tensor),
            lambda: pltpu.make_async_copy(src.at[j], dst_of(core).at[seq], recv.at[seq]).start(),
            lambda: remote(src.at[j], dst_of(core).at[seq], send.at[j], recv.at[seq], seq=peer, tensor=core).start(),
        )
        return 0

    lax.fori_loop(0, 16, body, 0)


def sent_to_workers(src, dst_of, send, recv):
    seq, _, tensor, _, _, _ = places()

    def body(j, _):
        peer, core = worker(tensor, j)
        pl.when(jnp.logical_not((peer == seq) & (core == tensor)))(
            lambda: remote(src.at[j], dst_of(core).at[seq], send.at[j], recv.at[seq], seq=peer, tensor=core).wait_send()
        )
        return 0

    lax.fori_loop(0, 16, body, 0)


def from_sources(src, dst_of, send, recv):
    seq, _, tensor, _, item_tensor, _ = places()
    dst = dst_of(tensor)

    def body(s, _):
        when_else(
            (s == seq) & (item_tensor == tensor),
            lambda: pltpu.make_async_copy(src.at[0], dst.at[s], recv.at[s]).wait(),
            lambda: remote(src.at[0], dst.at[s], send.at[0], recv.at[s], seq=s, tensor=item_tensor).wait_recv(),
        )
        return 0

    lax.fori_loop(0, 16, body, 0)


def to_source(s, src, dst, send, recv, what):
    seq, _, tensor, item_doc, item_tensor, item_head = places()
    slot = item_doc * 8 + item_head * 2 + tensor
    own = (s == seq) & (item_tensor == tensor)
    copy = lambda: remote(src, dst.at[slot], send.at[s], recv.at[slot], seq=s, tensor=item_tensor)
    if what == "start":
        when_else(
            own,
            lambda: pltpu.make_async_copy(src, dst.at[slot], recv.at[slot]).start(),
            lambda: copy().start(),
        )
    else:
        pl.when(jnp.logical_not(own))(lambda: copy().wait_send())


def from_workers(src, dst, send, recv):
    seq, _, tensor, _, _, _ = places()

    def body(j, _):
        peer, core = worker(tensor, j)
        when_else(
            (peer == seq) & (core == tensor),
            lambda: pltpu.make_async_copy(src, dst.at[j], recv.at[j]).wait(),
            lambda: remote(src, dst.at[j], send.at[0], recv.at[j], seq=peer, tensor=core).wait_recv(),
        )
        return 0

    lax.fori_loop(0, 16, body, 0)


def around(buf, send, recv, axis, size, step, src=None):
    me = lax.axis_index(axis)

    def copy(i):
        peer = lax.rem(me + i, size)
        from_ref = buf.at[me] if src is None else src.at[peer]
        return peer, from_ref

    def start(i, _):
        peer, from_ref = copy(i)
        remote(from_ref, buf.at[me], send.at[i], recv.at[me], **{axis: peer}).start()
        return 0

    def finish(i, _):
        peer, from_ref = copy(i)
        remote(from_ref, buf.at[peer], send.at[i], recv.at[peer], **{axis: peer}).wait()
        return 0

    lax.fori_loop(1, size, start if step == "start" else finish, 0)


def fold(x, op):
    return functools.reduce(op, [x[:, j * 128 : (j + 1) * 128] for j in range(x.shape[1] // 128)])


def column_of(row_values, rows):
    at = lax.broadcasted_iota(jnp.int32, (rows, 128), 0) == lax.broadcasted_iota(jnp.int32, (rows, 128), 1)
    return jnp.sum(jnp.where(at, row_values, 0.0), 1, keepdims=True)


def row_of(column):
    rows = column.shape[0]
    at = lax.broadcasted_iota(jnp.int32, (rows, 128), 0) == lax.broadcasted_iota(jnp.int32, (rows, 128), 1)
    return jnp.sum(jnp.where(at, column, 0.0), 0, keepdims=True)


def kernel(
    blk, len_ref, qi, gi, kvi, qe_ref, ids_ref,
    dq_out, dkv_out, qgrad_ref, loss_ref,
    q_all, g_all, kv_all, last_buf, part_buf, doc_buf, doc_all, logit_send, logit_recv, grad_send, grad_buf, ql,
    pg_own, pg_peer, s_ref, e_ref, d_ref, kt_ref, vt_ref, mx_ref, l_ref, t_ref, inv_ref, acc_ref, dq_s, keep, other, came, dkv_s,
    qs, qr, gs, gr, ks, kr, as_, ar, bs, br, dqs, dqr, dks, dkr, cs, cr, es, er, xs, xr, ds, dr, fs, fr, ps, pr,
):
    seq, dp, tensor, item_doc, item_tensor, item_head = places()
    rows = qi.shape[1]
    width = qe_ref.shape[1]
    scale = HD ** -0.5
    own_source = (item_tensor == tensor).astype(jnp.int32)

    def greetings(signal):
        def both(j, _):
            pl.when(jnp.logical_not((j == seq) & (item_tensor == tensor)))(lambda: signal(seq=j, tensor=item_tensor))
            peer, core = worker(tensor, j)
            pl.when(jnp.logical_not((peer == seq) & (core == tensor)))(lambda: signal(seq=peer, tensor=core))
            return 0

        lax.fori_loop(0, 16, both, 0)
        lax.fori_loop(1, SEQ, lambda i, c: (signal(seq=lax.rem(seq + i, SEQ)), c)[1], 0)
        lax.fori_loop(1, DP, lambda i, c: (signal(dp=lax.rem(dp + i, DP)), c)[1], 0)
        signal(tensor=1 - tensor)

    greet(greetings, 32 - 2 * own_source + (SEQ - 1) + (DP - 1) + 1)

    q_of, g_of, kv_of = lambda core: q_all, lambda core: g_all, lambda core: kv_all.at[core]
    kv_args, q_args, g_args = (kvi, kv_of, ks, kr), (qi, q_of, qs, qr), (gi, g_of, gs, gr)

    start = seq * rows
    length = [len_ref[0], len_ref[1]]
    row = lax.broadcasted_iota(jnp.int32, (rows, 1), 0) + start
    for j in range(16):
        at_last = row == length[j // 8] - 1
        picked = jnp.sum(jnp.where(at_last, qi[j].astype(F32), 0.0), 0, keepdims=True)
        ql[2 * j : 2 * j + 1, :] = picked[:, :HD]
        ql[2 * j + 1 : 2 * j + 2, :] = picked[:, HD:]
    last_buf[seq] = ql[...].astype(BF16)
    around(last_buf, as_, ar, "seq", SEQ, "start")
    qf = qe_ref[...].astype(F32)
    query_sq = jnp.sum(qf * qf, -1, keepdims=True)
    around(last_buf, as_, ar, "seq", SEQ, "finish")
    last = functools.reduce(jnp.add, [last_buf[i].astype(F32) for i in range(SEQ)]).astype(BF16)

    head_row = lax.broadcasted_iota(jnp.int32, (32, rows), 0)
    key_pos = lax.broadcasted_iota(jnp.int32, (32, rows), 1) + start
    scores = jnp.zeros((32, rows), F32)
    for j in range(8):
        term = lax.dot_general(last, kvi[2 * j], NT, preferred_element_type=F32)
        scores = jnp.where(head_row // GROUP == j, term, scores)
    visible = key_pos < jnp.where(head_row < 16, length[0], length[1])
    scores = jnp.where(visible, scores * scale, NEG_BIG)
    peak = jnp.max(scores, -1, keepdims=True)
    expw = jnp.where(visible, jnp.exp(scores - peak), 0.0)
    total = jnp.sum(expw, -1, keepdims=True)
    weights = expw.astype(BF16)
    mixed = jnp.zeros((32, HD), F32)
    wide_row = lax.broadcasted_iota(jnp.int32, (32, HD), 0)
    for j in range(8):
        term = lax.dot_general(weights, kvi[2 * j + 1], NN, preferred_element_type=F32)
        mixed = jnp.where(wide_row // GROUP == j, term, mixed)
    part_buf[seq, :32, :] = mixed
    part_buf[seq, 32:, :] = jnp.zeros((8, 128), F32)
    part_buf[seq, 32:33, :] = row_of(peak)
    part_buf[seq, 33:34, :] = row_of(total)
    around(part_buf, bs, br, "seq", SEQ, "start")
    around(part_buf, bs, br, "seq", SEQ, "finish")
    start_to_workers(*kv_args)
    start_to_workers(*q_args)
    start_to_workers(*g_args)
    peaks = [part_buf[i, 32:33, :] for i in range(SEQ)]
    top = functools.reduce(jnp.maximum, peaks)
    factors = [jnp.exp(p - top) for p in peaks]
    total = functools.reduce(jnp.add, [f * part_buf[i, 33:34, :] for i, f in enumerate(factors)])
    inv_total = 1.0 / jnp.where(total > 0.0, total, 1.0)
    pooled = functools.reduce(jnp.add, [column_of(f * inv_total, 32) * part_buf[i, :32, :] for i, f in enumerate(factors)])
    for d in range(2):
        for h in range(16):
            doc_buf[dp, d : d + 1, h * HD : (h + 1) * HD] = pooled[d * 16 + h : d * 16 + h + 1, :]
    around(doc_buf, cs, cr, "dp", DP, "start")
    around(doc_buf, cs, cr, "dp", DP, "finish")
    for i in range(DP):
        doc_all[2 * i : 2 * i + 2, :] = doc_buf[i]

    docs = doc_all[...]
    high = docs.astype(BF16)
    rest = docs - high.astype(F32)
    middle = rest.astype(BF16)
    low = (rest - middle.astype(F32)).astype(BF16)
    raw = functools.reduce(
        jnp.add, [lax.dot_general(qe_ref[...], x, NT, preferred_element_type=F32) for x in (low, middle, high)]
    )
    queries = qe_ref.shape[0]
    logit_send[...] = jnp.zeros_like(logit_send)
    logit_send[:queries, 0:8] = raw
    logit_send[:queries, 8:9] = query_sq
    logit_send[queries:, :] = jnp.broadcast_to(jnp.sum(docs * docs, -1, keepdims=True), (8, 128))
    exchange = remote(logit_send, logit_recv, ds, dr, tensor=1 - tensor)
    exchange.start()
    exchange.wait()
    both = logit_send[...] + logit_recv[...]
    query_norm = jnp.sqrt(both[:queries, 8:9] + EPS)
    doc_norm = jnp.sqrt(both[queries:, :] + EPS)
    norm_row = row_of(doc_norm[:, 0:1])
    ids = lax.broadcasted_iota(jnp.int32, (queries, 128), 1)
    real = ids < 8
    logits = jnp.where(real, both[:queries] / (query_norm * jnp.where(norm_row > 0.0, norm_row, 1.0)) / TAU, 0.0)
    counts = functools.reduce(
        jnp.add, [(ids_ref[:, c : c + 1] == ids).astype(F32) for c in range(1, ids_ref.shape[1])]
    )
    target = (ids_ref[:, 0:1] == ids).astype(F32)
    weighted = jnp.where(real, (1.0 + HARD_BOOST * counts) * jnp.exp(logits), 0.0)
    denom = jnp.sum(weighted, -1, keepdims=True)
    loss_rows = jnp.log(denom) - jnp.sum(target * logits, -1, keepdims=True)
    local_loss = jnp.sum(loss_rows, 0, keepdims=True)
    coef = weighted / denom - target
    inner_row = jnp.sum(coef * logits, 0, keepdims=True)
    doc_unit = docs / doc_norm[:, 0:1]
    by_norm = coef / query_norm
    one_lane = lax.broadcasted_iota(jnp.int32, (1, 128), 1)
    tail = jnp.where(one_lane == 8, local_loss, inner_row)
    for j in range(8):
        term = jnp.sum(by_norm[:, j : j + 1] * qf, 0, keepdims=True) / TAU
        grad_send[j // 2, j % 2 : j % 2 + 1, :width] = term
        grad_send[j // 2, j % 2 : j % 2 + 1, width:] = tail
    around(grad_buf, es, er, "dp", DP, "start", grad_send)
    qgrad_ref[...] = functools.reduce(jnp.add, [coef[:, j : j + 1] * doc_unit[j : j + 1, :] for j in range(8)]) / TAU
    grad_buf[dp] = grad_send[dp]
    around(grad_buf, es, er, "dp", DP, "finish", grad_send)
    summed = functools.reduce(jnp.add, [grad_buf[i] for i in range(DP)])
    tail = summed[0:1, width:]
    loss = jnp.sum(jnp.where(one_lane == 8, tail, 0.0), -1, keepdims=True) / (queries * DP)
    loss_ref[...] = jnp.broadcast_to(loss, loss_ref.shape)
    own = doc_buf[dp]
    for d in range(2):
        mine = one_lane == 2 * dp + d
        inner = jnp.sum(jnp.where(mine, tail, 0.0), -1, keepdims=True)
        norm = jnp.sum(jnp.where(mine, norm_row, 0.0), -1, keepdims=True)
        pooled_grad = (summed[d : d + 1, :width] - own[d : d + 1, :] / norm * inner) / norm
        for j in range(8):
            pg_own[8 * d + j] = pooled_grad[:, j * 256 : (j + 1) * 256]
    give = remote(pg_own, pg_peer, fs, fr, tensor=1 - tensor)
    give.start()

    from_sources(*kv_args)
    share = remote(kv_all.at[tensor], kv_all.at[tensor], ps, pr, tensor=1 - tensor)
    share.start()
    share.wait_send()
    remote(kv_all.at[tensor], kv_all.at[1 - tensor], ps, pr, tensor=1 - tensor).wait_recv()
    from_sources(*q_args)

    per = blk // rows
    blocks = SEQ // per
    lines = 2 * blk
    c2 = scale * math.log2(math.e)
    local = lax.rem(lax.broadcasted_iota(jnp.int32, (lines, blk), 0), blk)
    diagonal = local >= lax.broadcasted_iota(jnp.int32, (lines, blk), 1)
    line = lax.rem(lax.broadcasted_iota(jnp.int32, (lines, 1), 0), blk)

    def stacked(ref, i):
        x = ref[pl.ds(i * per, per)].reshape(blk, 2 * HD)
        return jnp.concatenate([x[:, :HD], x[:, HD:]], 0)

    def keys(kind, c):
        return kv_all[kind, pl.ds(c * per, per)].reshape(blk, HD)

    def forward(i, _):
        q = stacked(q_all, i)
        first = i * (i + 1) // 2
        s = lax.dot_general(q, keys(0, i), NT, preferred_element_type=F32)
        s = jnp.where(diagonal, s, NEG_BIG)
        mx_ref[...] = fold(s, jnp.maximum)
        s_ref[i] = s

        def score(c, _):
            s = lax.dot_general(q, keys(0, c), NT, preferred_element_type=F32)
            mx_ref[...] = jnp.maximum(mx_ref[...], fold(s, jnp.maximum))
            s_ref[c] = s
            return 0

        lax.fori_loop(0, i, score, 0)
        m = jnp.max(mx_ref[...], -1, keepdims=True) * c2
        l_ref[...] = jnp.zeros_like(l_ref)

        def weigh(c, _):
            e = jnp.exp2(s_ref[c] * c2 - m)
            l_ref[...] += fold(e, jnp.add)
            e_ref[first + c] = e.astype(BF16)
            return 0

        lax.fori_loop(0, i + 1, weigh, 0)
        inv_ref[i] = jnp.broadcast_to(1.0 / jnp.sum(l_ref[...], -1, keepdims=True), (lines, 128))
        return 0

    lax.fori_loop(0, blocks, forward, 0)

    give.wait()
    slot = item_doc * 8 + item_head * 2 + tensor
    extra = jnp.where(item_tensor == tensor, pg_own[slot], pg_peer[slot])
    doc_length = jnp.where(item_doc == 0, length[0], length[1])
    half_line = lax.broadcasted_iota(jnp.int32, (lines, 1), 0) < blk
    extra = jnp.where(half_line, extra[:, :HD], extra[:, HD:])
    kt_ref[...] = jnp.zeros_like(kt_ref)
    vt_ref[...] = jnp.zeros_like(vt_ref)
    from_sources(*g_args)

    def send_keys(i, what):
        swap = remote(other.at[i], came.at[i], xs.at[i], xr.at[i], tensor=1 - tensor)
        if what == "finish":
            swap.wait()
            dkv_s[pl.ds(i * per, per)] = (keep[i] + came[i]).astype(BF16).reshape(per, rows, HD)

            def one(p, _):
                s = i * per + p
                to_source(s, dkv_s.at[s], dkv_out, dks, dkr, "start")
                return 0

            lax.fori_loop(0, per, one, 0)
        else:
            swap.start()

    def backward(n, _):
        i = blocks - 1 - n
        first = i * (i + 1) // 2
        q = stacked(q_all, i)
        at = line + i * blk
        g = jnp.where(at < doc_length, stacked(g_all, i).astype(F32), 0.0)
        g = (g + jnp.where(at == doc_length - 1, extra, 0.0)).astype(BF16)
        t_ref[...] = jnp.zeros_like(t_ref)

        def weigh(c, _):
            dp_ = lax.dot_general(g, keys(1, c), NT, preferred_element_type=F32)
            t_ref[...] += fold(e_ref[first + c].astype(F32) * dp_, jnp.add)
            d_ref[c] = dp_.astype(BF16)
            return 0

        lax.fori_loop(0, i + 1, weigh, 0)
        inv = inv_ref[i][:, 0:1]
        d_vec = (jnp.sum(t_ref[...], -1, keepdims=True) * inv).astype(BF16)
        gt = (g.astype(F32) * inv).astype(BF16).T
        qt = (q.astype(F32) * inv).astype(BF16).T
        acc_ref[...] = jnp.zeros_like(acc_ref)

        def spread(c, _):
            ks_ = pl.ds(pl.multiple_of(c * blk, blk), blk)
            e = e_ref[first + c]
            grad_s = e * (d_ref[c] - d_vec)
            vt_ref[:, ks_] += lax.dot_general(gt, e, NN, preferred_element_type=F32)
            kt_ref[:, ks_] += lax.dot_general(qt, grad_s, NN, preferred_element_type=F32)
            acc_ref[...] += lax.dot_general(grad_s, keys(0, c), NN, preferred_element_type=F32)
            return 0

        lax.fori_loop(0, i + 1, spread, 0)
        dq = (acc_ref[...] * (inv * scale)).astype(BF16)
        dq_s[pl.ds(i * per, per)] = jnp.concatenate([dq[:blk], dq[blk:]], 1).reshape(per, rows, 2 * HD)

        def one(p, _):
            s = i * per + p
            to_source(s, dq_s.at[s], dq_out, dqs, dqr, "start")
            return 0

        lax.fori_loop(0, per, one, 0)
        here = pl.ds(pl.multiple_of(i * blk, blk), blk)
        dk = kt_ref[:, here].T * scale
        dv = vt_ref[:, here].T
        keep[i] = jnp.where(tensor == 0, dk, dv)
        other[i] = jnp.where(tensor == 0, dv, dk)
        send_keys(i, "start")
        pl.when(n > 0)(lambda: send_keys(i + 1, "finish"))
        return 0

    lax.fori_loop(0, blocks, backward, 0)
    send_keys(0, "finish")

    from_workers(dq_s.at[0], dq_out, dqs, dqr)
    from_workers(dkv_s.at[0], dkv_out, dks, dkr)

    def sent(s, _):
        to_source(s, dq_s.at[s], dq_out, dqs, dqr, "sent")
        to_source(s, dkv_s.at[s], dkv_out, dks, dkr, "sent")
        return 0

    lax.fori_loop(0, SEQ, sent, 0)
    for args in (kv_args, q_args, g_args):
        sent_to_workers(*args)


def on_device(q_proj, k_proj, v_proj, lm_cotangent, query_emb, doc_lengths, positive_ids, hard_ids):
    rows, docs, half = q_proj.shape
    heads = k_proj.shape[2] // HD
    queries, width = query_emb.shape
    blk = 4 * rows
    blocks, lines = SEQ * rows // blk, 2 * blk
    vmem = pl.BlockSpec(memory_space=pltpu.VMEM)
    smem = pl.BlockSpec(memory_space=pltpu.SMEM)
    dma = pltpu.SemaphoreType.DMA

    def query_parts(x):
        return x.reshape(rows, docs, heads, 2, 2 * HD).transpose(1, 2, 3, 0, 4).reshape(16, rows, 2 * HD)

    pair = jnp.stack([x.reshape(rows, docs, heads, HD) for x in (k_proj, v_proj)], 3)
    key_parts = pair.transpose(1, 2, 3, 0, 4).reshape(16, rows, HD)
    ids = jnp.concatenate((positive_ids[:, None], hard_ids), 1)
    wide, slim = (16, rows, 2 * HD), (16, rows, HD)
    dq, dkv, query_grad, loss = pl.pallas_call(
        functools.partial(kernel, blk),
        name="whole",
        out_shape=[
            jax.ShapeDtypeStruct(wide, BF16),
            jax.ShapeDtypeStruct(slim, BF16),
            jax.ShapeDtypeStruct((queries, width), F32),
            jax.ShapeDtypeStruct((8, 128), F32),
        ],
        in_specs=[smem] + [vmem] * 5,
        out_specs=[vmem] * 4,
        scratch_shapes=[
            pltpu.VMEM(wide, BF16),
            pltpu.VMEM(wide, BF16),
            pltpu.VMEM((2,) + slim, BF16),
            pltpu.VMEM((SEQ, 32, HD), BF16),
            pltpu.VMEM((SEQ, 40, HD), F32),
            pltpu.VMEM((DP, 2, width), F32),
            pltpu.VMEM((8, width), F32),
            pltpu.VMEM((queries + 8, 128), F32),
            pltpu.VMEM((queries + 8, 128), F32),
            pltpu.VMEM((DP, 2, width + 128), F32),
            pltpu.VMEM((DP, 2, width + 128), F32),
            pltpu.VMEM((32, HD), F32),
            pltpu.VMEM((16, 1, 2 * HD), F32),
            pltpu.VMEM((16, 1, 2 * HD), F32),
            pltpu.VMEM((blocks, lines, blk), F32),
            pltpu.VMEM((blocks * (blocks + 1) // 2, lines, blk), BF16),
            pltpu.VMEM((blocks, lines, blk), BF16),
            pltpu.VMEM((HD, blocks * blk), F32),
            pltpu.VMEM((HD, blocks * blk), F32),
            pltpu.VMEM((lines, 128), F32),
            pltpu.VMEM((lines, 128), F32),
            pltpu.VMEM((lines, 128), F32),
            pltpu.VMEM((blocks, lines, 128), F32),
            pltpu.VMEM((lines, 128), F32),
            pltpu.VMEM(wide, BF16),
            pltpu.VMEM((blocks, blk, HD), F32),
            pltpu.VMEM((blocks, blk, HD), F32),
            pltpu.VMEM((blocks, blk, HD), F32),
            pltpu.VMEM(slim, BF16),
        ]
        + [dma((16,))] * 14
        + [dma((DP,))] * 4
        + [dma((blocks,))] * 2
        + [dma] * 6,
        compiler_params=pltpu.CompilerParams(collective_id=0, has_side_effects=True, vmem_limit_bytes=56 * 2**20),
    )(doc_lengths, query_parts(q_proj), query_parts(lm_cotangent), key_parts, query_emb, ids)
    grad_q = dq.reshape(docs, heads * 2, rows, 2 * HD).transpose(2, 0, 1, 3).reshape(rows, docs, half)
    key_grads = dkv.reshape(docs, heads, 2, rows, HD).transpose(2, 3, 0, 1, 4).reshape(2, rows, docs, heads * HD)
    return grad_q, key_grads[0], key_grads[1], query_grad, loss[0, 0]


def solution(mesh):
    return jax.shard_map(
        on_device,
        mesh=mesh,
        in_specs=(
            P("seq", "dp", "tensor"),
            P("seq", "dp", "tensor"),
            P("seq", "dp", "tensor"),
            P("seq", "dp", "tensor"),
            P("dp", "tensor"),
            P("dp"),
            P("dp"),
            P("dp", None),
        ),
        out_specs=(
            P("seq", "dp", "tensor"),
            P("seq", "dp", "tensor"),
            P("seq", "dp", "tensor"),
            P("dp", "tensor"),
            P(),
        ),
        check_vma=False,
    )
```

```python
import functools
import math

import jax
import jax.numpy as jnp
from jax import lax
from jax.experimental import pallas as pl
from jax.experimental.pallas import tpu as pltpu
from jax.sharding import PartitionSpec as P

QH = 32
KVH = 8
HD = 128
TAU = 0.02
HARD_BOOST = 3.0
EPS = 1e-06
NEG_BIG = -1e30
SEQ = 16
DP = 4
GROUP = QH // KVH
MESH = pl.DeviceIdType.MESH
NT = (((1,), (1,)), ((), ()))
NN = (((1,), (0,)), ((), ()))
F32 = jnp.float32
BF16 = jnp.bfloat16


def places():
    seq, dp, tensor = lax.axis_index("seq"), lax.axis_index("dp"), lax.axis_index("tensor")
    return seq, dp, tensor, seq // 8, lax.rem(seq // 4, 2), lax.rem(seq, 4)


def remote(src, dst, send, recv, **device):
    return pltpu.make_async_remote_copy(
        src_ref=src, dst_ref=dst, send_sem=send, recv_sem=recv, device_id=device, device_id_type=MESH
    )


def worker(tensor, j):
    return (j // 8) * 8 + tensor * 4 + lax.rem(j // 2, 4), lax.rem(j, 2)


def greet(send_to, count):
    barrier = pltpu.get_barrier_semaphore()
    send_to(lambda **device: pl.semaphore_signal(barrier, inc=1, device_id=device, device_id_type=MESH))
    pl.semaphore_wait(barrier, count)


def when_else(cond, yes, no):
    pl.when(cond)(yes)
    pl.when(jnp.logical_not(cond))(no)


def start_to_workers(src_of, dst_of, send, recv, first=0, end=8):
    seq, _, tensor, _, _, _ = places()

    def body(n, _):
        head = lax.rem(seq + 2 + n, 4)
        doc = lax.rem(seq // 8 + 1 + n // 4, 2)
        for core in range(2):
            j = doc * 8 + head * 2 + core
            peer, _ = worker(tensor, j)
            src, dst = src_of(j, core), dst_of(core)
            when_else(
                (peer == seq) & (core == tensor),
                lambda: pltpu.make_async_copy(src, dst.at[seq], recv.at[seq]).start(),
                lambda: remote(src, dst.at[seq], send.at[j], recv.at[seq], seq=peer, tensor=core).start(),
            )
        return 0

    lax.fori_loop(first, end, body, 0)


def sent_to_workers(src_of, dst_of, send, recv):
    seq, _, tensor, _, _, _ = places()

    def body(n, _):
        for core in range(2):
            j = 2 * n + core
            peer, _ = worker(tensor, j)
            src, dst = src_of(j, core), dst_of(core)
            pl.when(jnp.logical_not((peer == seq) & (core == tensor)))(
                lambda: remote(src, dst.at[seq], send.at[j], recv.at[seq], seq=peer, tensor=core).wait_send()
            )
        return 0

    lax.fori_loop(0, 8, body, 0)


def from_sources(src_of, dst_of, send, recv):
    seq, _, tensor, _, item_tensor, _ = places()
    src, dst = src_of(0, 0), dst_of(tensor)

    def body(s, _):
        when_else(
            (s == seq) & (item_tensor == tensor),
            lambda: pltpu.make_async_copy(src, dst.at[s], recv.at[s]).wait(),
            lambda: remote(src, dst.at[s], send.at[0], recv.at[s], seq=s, tensor=item_tensor).wait_recv(),
        )
        return 0

    lax.fori_loop(0, 16, body, 0)


def to_source(s, src, dst, send, recv, what):
    seq, _, tensor, item_doc, item_tensor, item_head = places()
    slot = item_doc * 8 + item_head * 2 + tensor
    own = (s == seq) & (item_tensor == tensor)
    copy = lambda: remote(src, dst.at[slot], send.at[s], recv.at[slot], seq=s, tensor=item_tensor)
    if what == "start":
        when_else(
            own,
            lambda: pltpu.make_async_copy(src, dst.at[slot], recv.at[slot]).start(),
            lambda: copy().start(),
        )
    else:
        pl.when(jnp.logical_not(own))(lambda: copy().wait_send())


def from_workers(src, dst, send, recv):
    seq, _, tensor, _, _, _ = places()

    def body(j, _):
        peer, core = worker(tensor, j)
        when_else(
            (peer == seq) & (core == tensor),
            lambda: pltpu.make_async_copy(src, dst.at[j], recv.at[j]).wait(),
            lambda: remote(src, dst.at[j], send.at[0], recv.at[j], seq=peer, tensor=core).wait_recv(),
        )
        return 0

    lax.fori_loop(0, 16, body, 0)


def around(buf, send, recv, axis, size, step, src=None):
    me = lax.axis_index(axis)

    def copy(i):
        peer = lax.rem(me + i, size)
        from_ref = buf.at[me] if src is None else src.at[peer]
        return peer, from_ref

    def start(i, _):
        peer, from_ref = copy(i)
        remote(from_ref, buf.at[me], send.at[i], recv.at[me], **{axis: peer}).start()
        return 0

    def finish(i, _):
        peer, from_ref = copy(i)
        remote(from_ref, buf.at[peer], send.at[i], recv.at[peer], **{axis: peer}).wait()
        return 0

    lax.fori_loop(1, size, start if step == "start" else finish, 0)


def fold(x, op):
    return functools.reduce(op, [x[:, j * 128 : (j + 1) * 128] for j in range(x.shape[1] // 128)])


def column_of(row_values, rows):
    at = lax.broadcasted_iota(jnp.int32, (rows, 128), 0) == lax.broadcasted_iota(jnp.int32, (rows, 128), 1)
    return jnp.sum(jnp.where(at, row_values, 0.0), 1, keepdims=True)


def row_of(column):
    rows = column.shape[0]
    at = lax.broadcasted_iota(jnp.int32, (rows, 128), 0) == lax.broadcasted_iota(jnp.int32, (rows, 128), 1)
    return jnp.sum(jnp.where(at, column, 0.0), 0, keepdims=True)


def kernel(
    blk, len_ref, qi, gi, ki, vi, qe_ref, ids_ref,
    dq_out, dkv_out, qgrad_ref, loss_ref,
    q_all, g_all, kv_all, last_buf, part_buf, doc_buf, doc_all, logit_send, logit_recv, grad_send, grad_buf, ql,
    pg_own, pg_peer, s_ref, e_ref, d_ref, kt_ref, vt_ref, mx_ref, l_ref, t_ref, inv_ref, acc_ref, dq_s, keep, other, came, dkv_s,
    qs, qr, gs, gr, ks, kr, as_, ar, bs, br, dqs, dqr, dks, dkr, cs, cr, es, er, xs, xr, ds, dr, fs, fr, ps, pr,
):
    seq, dp, tensor, item_doc, item_tensor, item_head = places()
    rows = qi.shape[1]
    width = qe_ref.shape[1]
    scale = HD ** -0.5
    own_source = (item_tensor == tensor).astype(jnp.int32)

    def greetings(signal):
        def both(j, _):
            pl.when(jnp.logical_not((j == seq) & (item_tensor == tensor)))(lambda: signal(seq=j, tensor=item_tensor))
            peer, core = worker(tensor, j)
            pl.when(jnp.logical_not((peer == seq) & (core == tensor)))(lambda: signal(seq=peer, tensor=core))
            return 0

        lax.fori_loop(0, 16, both, 0)
        lax.fori_loop(1, SEQ, lambda i, c: (signal(seq=lax.rem(seq + i, SEQ)), c)[1], 0)
        lax.fori_loop(1, DP, lambda i, c: (signal(dp=lax.rem(dp + i, DP)), c)[1], 0)
        signal(tensor=1 - tensor)

    greet(greetings, 32 - 2 * own_source + (SEQ - 1) + (DP - 1) + 1)

    q_of, g_of, kv_of = lambda core: q_all, lambda core: g_all, lambda core: kv_all.at[core]
    kv_args = (lambda j, core: (ki, vi)[core].at[j // 2], kv_of, ks, kr)
    q_args = (lambda j, core: qi.at[j], q_of, qs, qr)
    g_args = (lambda j, core: gi.at[j], g_of, gs, gr)

    start = seq * rows
    length = [len_ref[0], len_ref[1]]
    row = lax.broadcasted_iota(jnp.int32, (rows, 1), 0) + start
    for j in range(16):
        at_last = row == length[j // 8] - 1
        picked = jnp.sum(jnp.where(at_last, qi[j].astype(F32), 0.0), 0, keepdims=True)
        ql[2 * j : 2 * j + 1, :] = picked[:, :HD]
        ql[2 * j + 1 : 2 * j + 2, :] = picked[:, HD:]
    last_buf[seq] = ql[...].astype(BF16)
    around(last_buf, as_, ar, "seq", SEQ, "start")
    start_to_workers(*kv_args)
    qf = qe_ref[...].astype(F32)
    query_sq = jnp.sum(qf * qf, -1, keepdims=True)
    around(last_buf, as_, ar, "seq", SEQ, "finish")
    last = functools.reduce(jnp.add, [last_buf[i].astype(F32) for i in range(SEQ)]).astype(BF16)

    head_row = lax.broadcasted_iota(jnp.int32, (32, rows), 0)
    key_pos = lax.broadcasted_iota(jnp.int32, (32, rows), 1) + start
    scores = jnp.zeros((32, rows), F32)
    for j in range(8):
        term = lax.dot_general(last, ki[j], NT, preferred_element_type=F32)
        scores = jnp.where(head_row // GROUP == j, term, scores)
    visible = key_pos < jnp.where(head_row < 16, length[0], length[1])
    scores = jnp.where(visible, scores * scale, NEG_BIG)
    peak = jnp.max(scores, -1, keepdims=True)
    expw = jnp.where(visible, jnp.exp(scores - peak), 0.0)
    total = jnp.sum(expw, -1, keepdims=True)
    weights = expw.astype(BF16)
    mixed = jnp.zeros((32, HD), F32)
    wide_row = lax.broadcasted_iota(jnp.int32, (32, HD), 0)
    for j in range(8):
        term = lax.dot_general(weights, vi[j], NN, preferred_element_type=F32)
        mixed = jnp.where(wide_row // GROUP == j, term, mixed)
    part_buf[seq, :32, :] = mixed
    part_buf[seq, 32:, :] = jnp.zeros((8, 128), F32)
    part_buf[seq, 32:33, :] = row_of(peak)
    part_buf[seq, 33:34, :] = row_of(total)
    around(part_buf, bs, br, "seq", SEQ, "start")
    start_to_workers(*q_args, 0, 4)
    around(part_buf, bs, br, "seq", SEQ, "finish")
    peaks = [part_buf[i, 32:33, :] for i in range(SEQ)]
    top = functools.reduce(jnp.maximum, peaks)
    factors = [jnp.exp(p - top) for p in peaks]
    total = functools.reduce(jnp.add, [f * part_buf[i, 33:34, :] for i, f in enumerate(factors)])
    inv_total = 1.0 / jnp.where(total > 0.0, total, 1.0)
    pooled = functools.reduce(jnp.add, [column_of(f * inv_total, 32) * part_buf[i, :32, :] for i, f in enumerate(factors)])
    for d in range(2):
        for h in range(16):
            doc_buf[dp, d : d + 1, h * HD : (h + 1) * HD] = pooled[d * 16 + h : d * 16 + h + 1, :]
    around(doc_buf, cs, cr, "dp", DP, "start")
    start_to_workers(*q_args, 4, 8)
    around(doc_buf, cs, cr, "dp", DP, "finish")
    for i in range(DP):
        doc_all[2 * i : 2 * i + 2, :] = doc_buf[i]

    docs = doc_all[...]
    high = docs.astype(BF16)
    rest = docs - high.astype(F32)
    middle = rest.astype(BF16)
    low = (rest - middle.astype(F32)).astype(BF16)
    raw = functools.reduce(
        jnp.add, [lax.dot_general(qe_ref[...], x, NT, preferred_element_type=F32) for x in (low, middle, high)]
    )
    queries = qe_ref.shape[0]
    logit_send[...] = jnp.zeros_like(logit_send)
    logit_send[:queries, 0:8] = raw
    logit_send[:queries, 8:9] = query_sq
    logit_send[queries:, :] = jnp.broadcast_to(jnp.sum(docs * docs, -1, keepdims=True), (8, 128))
    exchange = remote(logit_send, logit_recv, ds, dr, tensor=1 - tensor)
    exchange.start()
    exchange.wait()
    both = logit_send[...] + logit_recv[...]
    query_norm = jnp.sqrt(both[:queries, 8:9] + EPS)
    doc_norm = jnp.sqrt(both[queries:, :] + EPS)
    norm_row = row_of(doc_norm[:, 0:1])
    ids = lax.broadcasted_iota(jnp.int32, (queries, 128), 1)
    real = ids < 8
    logits = jnp.where(real, both[:queries] / (query_norm * jnp.where(norm_row > 0.0, norm_row, 1.0)) / TAU, 0.0)
    counts = functools.reduce(
        jnp.add, [(ids_ref[:, c : c + 1] == ids).astype(F32) for c in range(1, ids_ref.shape[1])]
    )
    target = (ids_ref[:, 0:1] == ids).astype(F32)
    weighted = jnp.where(real, (1.0 + HARD_BOOST * counts) * jnp.exp(logits), 0.0)
    denom = jnp.sum(weighted, -1, keepdims=True)
    loss_rows = jnp.log(denom) - jnp.sum(target * logits, -1, keepdims=True)
    local_loss = jnp.sum(loss_rows, 0, keepdims=True)
    coef = weighted / denom - target
    inner_row = jnp.sum(coef * logits, 0, keepdims=True)
    doc_unit = docs / doc_norm[:, 0:1]
    by_norm = coef / query_norm
    one_lane = lax.broadcasted_iota(jnp.int32, (1, 128), 1)
    tail = jnp.where(one_lane == 8, local_loss, inner_row)
    for j in range(8):
        term = jnp.sum(by_norm[:, j : j + 1] * qf, 0, keepdims=True) / TAU
        grad_send[j // 2, j % 2 : j % 2 + 1, :width] = term
        grad_send[j // 2, j % 2 : j % 2 + 1, width:] = tail
    around(grad_buf, es, er, "dp", DP, "start", grad_send)
    start_to_workers(*g_args, 0, 4)
    qgrad_ref[...] = functools.reduce(jnp.add, [coef[:, j : j + 1] * doc_unit[j : j + 1, :] for j in range(8)]) / TAU
    grad_buf[dp] = grad_send[dp]
    around(grad_buf, es, er, "dp", DP, "finish", grad_send)
    summed = functools.reduce(jnp.add, [grad_buf[i] for i in range(DP)])
    tail = summed[0:1, width:]
    loss = jnp.sum(jnp.where(one_lane == 8, tail, 0.0), -1, keepdims=True) / (queries * DP)
    loss_ref[...] = loss
    own = doc_buf[dp]
    for d in range(2):
        mine = one_lane == 2 * dp + d
        inner = jnp.sum(jnp.where(mine, tail, 0.0), -1, keepdims=True)
        norm = jnp.sum(jnp.where(mine, norm_row, 0.0), -1, keepdims=True)
        pooled_grad = (summed[d : d + 1, :width] - own[d : d + 1, :] / norm * inner) / norm
        for j in range(8):
            pg_own[8 * d + j] = pooled_grad[:, j * 256 : (j + 1) * 256]
    give = remote(pg_own, pg_peer, fs, fr, tensor=1 - tensor)
    give.start()
    start_to_workers(*g_args, 4, 8)

    from_sources(*kv_args)
    share = remote(kv_all.at[tensor], kv_all.at[tensor], ps, pr, tensor=1 - tensor)
    share.start()
    share.wait_send()
    remote(kv_all.at[tensor], kv_all.at[1 - tensor], ps, pr, tensor=1 - tensor).wait_recv()
    from_sources(*q_args)

    per = blk // rows
    blocks = SEQ // per
    lines = 2 * blk
    c2 = scale * math.log2(math.e)
    local = lax.rem(lax.broadcasted_iota(jnp.int32, (lines, blk), 0), blk)
    diagonal = local >= lax.broadcasted_iota(jnp.int32, (lines, blk), 1)
    line = lax.rem(lax.broadcasted_iota(jnp.int32, (lines, 1), 0), blk)

    def stacked(ref, i):
        x = ref[pl.ds(i * per, per)].reshape(blk, 2 * HD)
        return jnp.concatenate([x[:, :HD], x[:, HD:]], 0)

    def keys(kind, c):
        return kv_all[kind, pl.ds(c * per, per)].reshape(blk, HD)

    def forward(i, _):
        q = stacked(q_all, i)
        first = i * (i + 1) // 2
        s = lax.dot_general(q, keys(0, i), NT, preferred_element_type=F32)
        s = jnp.where(diagonal, s, NEG_BIG)
        mx_ref[...] = fold(s, jnp.maximum)
        s_ref[i] = s

        def score(c, _):
            s = lax.dot_general(q, keys(0, c), NT, preferred_element_type=F32)
            mx_ref[...] = jnp.maximum(mx_ref[...], fold(s, jnp.maximum))
            s_ref[c] = s
            return 0

        lax.fori_loop(0, i, score, 0)
        m = jnp.max(mx_ref[...], -1, keepdims=True) * c2
        l_ref[...] = jnp.zeros_like(l_ref)

        def weigh(c, _):
            e = jnp.exp2(s_ref[c] * c2 - m)
            l_ref[...] += fold(e, jnp.add)
            e_ref[first + c] = e.astype(BF16)
            return 0

        lax.fori_loop(0, i + 1, weigh, 0)
        inv_ref[i] = jnp.broadcast_to(1.0 / jnp.sum(l_ref[...], -1, keepdims=True), (lines, 128))
        return 0

    lax.fori_loop(0, blocks, forward, 0)

    give.wait()
    slot = item_doc * 8 + item_head * 2 + tensor
    extra = jnp.where(item_tensor == tensor, pg_own[slot], pg_peer[slot])
    doc_length = jnp.where(item_doc == 0, length[0], length[1])
    half_line = lax.broadcasted_iota(jnp.int32, (lines, 1), 0) < blk
    extra = jnp.where(half_line, extra[:, :HD], extra[:, HD:])
    kt_ref[...] = jnp.zeros_like(kt_ref)
    vt_ref[...] = jnp.zeros_like(vt_ref)
    from_sources(*g_args)

    def send_keys(i, what):
        swap = remote(other.at[i], came.at[i], xs.at[i], xr.at[i], tensor=1 - tensor)
        if what == "finish":
            swap.wait()
            dkv_s[pl.ds(i * per, per)] = (keep[i] + came[i]).astype(BF16).reshape(per, rows, HD)

            def one(p, _):
                s = i * per + p
                to_source(s, dkv_s.at[s], dkv_out, dks, dkr, "start")
                return 0

            lax.fori_loop(0, per, one, 0)
        else:
            swap.start()

    def backward(n, _):
        i = blocks - 1 - n
        first = i * (i + 1) // 2
        q = stacked(q_all, i)
        at = line + i * blk
        g = jnp.where(at < doc_length, stacked(g_all, i).astype(F32), 0.0)
        g = (g + jnp.where(at == doc_length - 1, extra, 0.0)).astype(BF16)
        t_ref[...] = jnp.zeros_like(t_ref)

        def weigh(c, _):
            dp_ = lax.dot_general(g, keys(1, c), NT, preferred_element_type=F32)
            t_ref[...] += fold(e_ref[first + c].astype(F32) * dp_, jnp.add)
            d_ref[c] = dp_.astype(BF16)
            return 0

        lax.fori_loop(0, i + 1, weigh, 0)
        inv = inv_ref[i][:, 0:1]
        d_vec = (jnp.sum(t_ref[...], -1, keepdims=True) * inv).astype(BF16)
        gt = (g.astype(F32) * inv).astype(BF16).T
        qt = (q.astype(F32) * inv).astype(BF16).T
        acc_ref[...] = jnp.zeros_like(acc_ref)

        def spread(c, _):
            ks_ = pl.ds(pl.multiple_of(c * blk, blk), blk)
            e = e_ref[first + c]
            grad_s = e * (d_ref[c] - d_vec)
            vt_ref[:, ks_] += lax.dot_general(gt, e, NN, preferred_element_type=F32)
            kt_ref[:, ks_] += lax.dot_general(qt, grad_s, NN, preferred_element_type=F32)
            acc_ref[...] += lax.dot_general(grad_s, keys(0, c), NN, preferred_element_type=F32)
            return 0

        lax.fori_loop(0, i + 1, spread, 0)
        dq = (acc_ref[...] * (inv * scale)).astype(BF16)
        dq_s[pl.ds(i * per, per)] = jnp.concatenate([dq[:blk], dq[blk:]], 1).reshape(per, rows, 2 * HD)

        def one(p, _):
            s = i * per + p
            to_source(s, dq_s.at[s], dq_out, dqs, dqr, "start")
            return 0

        lax.fori_loop(0, per, one, 0)
        here = pl.ds(pl.multiple_of(i * blk, blk), blk)
        dk = kt_ref[:, here].T * scale
        dv = vt_ref[:, here].T
        keep[i] = jnp.where(tensor == 0, dk, dv)
        other[i] = jnp.where(tensor == 0, dv, dk)
        send_keys(i, "start")
        pl.when(n > 0)(lambda: send_keys(i + 1, "finish"))
        return 0

    lax.fori_loop(0, blocks, backward, 0)
    send_keys(0, "finish")

    from_workers(dq_s.at[0], dq_out, dqs, dqr)
    from_workers(dkv_s.at[0], dkv_out, dks, dkr)

    def sent(s, _):
        to_source(s, dq_s.at[s], dq_out, dqs, dqr, "sent")
        to_source(s, dkv_s.at[s], dkv_out, dks, dkr, "sent")
        return 0

    lax.fori_loop(0, SEQ, sent, 0)
    for args in (kv_args, q_args, g_args):
        sent_to_workers(*args)


def on_device(q_proj, k_proj, v_proj, lm_cotangent, query_emb, doc_lengths, positive_ids, hard_ids):
    rows, docs, half = q_proj.shape
    heads = k_proj.shape[2] // HD
    queries, width = query_emb.shape
    blk = 4 * rows
    blocks, lines = SEQ * rows // blk, 2 * blk
    vmem = pl.BlockSpec(memory_space=pltpu.VMEM)
    smem = pl.BlockSpec(memory_space=pltpu.SMEM)
    dma = pltpu.SemaphoreType.DMA

    def query_parts(x):
        return x.reshape(rows, docs, heads, 2, 2 * HD).transpose(1, 2, 3, 0, 4).reshape(16, rows, 2 * HD)

    def key_parts(x):
        return x.reshape(rows, docs, heads, HD).transpose(1, 2, 0, 3).reshape(8, rows, HD)

    ids = jnp.concatenate((positive_ids[:, None], hard_ids), 1)
    wide, slim = (16, rows, 2 * HD), (16, rows, HD)
    dq, dkv, query_grad, loss = pl.pallas_call(
        functools.partial(kernel, blk),
        name="whole",
        out_shape=[
            jax.ShapeDtypeStruct(wide, BF16),
            jax.ShapeDtypeStruct(slim, BF16),
            jax.ShapeDtypeStruct((queries, width), F32),
            jax.ShapeDtypeStruct((1, 1), F32),
        ],
        in_specs=[smem] + [vmem] * 6,
        out_specs=[vmem] * 4,
        scratch_shapes=[
            pltpu.VMEM(wide, BF16),
            pltpu.VMEM(wide, BF16),
            pltpu.VMEM((2,) + slim, BF16),
            pltpu.VMEM((SEQ, 32, HD), BF16),
            pltpu.VMEM((SEQ, 40, HD), F32),
            pltpu.VMEM((DP, 2, width), F32),
            pltpu.VMEM((8, width), F32),
            pltpu.VMEM((queries + 8, 128), F32),
            pltpu.VMEM((queries + 8, 128), F32),
            pltpu.VMEM((DP, 2, width + 128), F32),
            pltpu.VMEM((DP, 2, width + 128), F32),
            pltpu.VMEM((32, HD), F32),
            pltpu.VMEM((16, 1, 2 * HD), F32),
            pltpu.VMEM((16, 1, 2 * HD), F32),
            pltpu.VMEM((blocks, lines, blk), F32),
            pltpu.VMEM((blocks * (blocks + 1) // 2, lines, blk), BF16),
            pltpu.VMEM((blocks, lines, blk), BF16),
            pltpu.VMEM((HD, blocks * blk), F32),
            pltpu.VMEM((HD, blocks * blk), F32),
            pltpu.VMEM((lines, 128), F32),
            pltpu.VMEM((lines, 128), F32),
            pltpu.VMEM((lines, 128), F32),
            pltpu.VMEM((blocks, lines, 128), F32),
            pltpu.VMEM((lines, 128), F32),
            pltpu.VMEM(wide, BF16),
            pltpu.VMEM((blocks, blk, HD), F32),
            pltpu.VMEM((blocks, blk, HD), F32),
            pltpu.VMEM((blocks, blk, HD), F32),
            pltpu.VMEM(slim, BF16),
        ]
        + [dma((16,))] * 14
        + [dma((DP,))] * 4
        + [dma((blocks,))] * 2
        + [dma] * 6,
        compiler_params=pltpu.CompilerParams(collective_id=0, has_side_effects=True, vmem_limit_bytes=56 * 2**20),
    )(doc_lengths, query_parts(q_proj), query_parts(lm_cotangent), key_parts(k_proj), key_parts(v_proj), query_emb, ids)
    grad_q = dq.reshape(docs, heads * 2, rows, 2 * HD).transpose(2, 0, 1, 3).reshape(rows, docs, half)
    key_grads = dkv.reshape(docs, heads, 2, rows, HD).transpose(2, 3, 0, 1, 4).reshape(2, rows, docs, heads * HD)
    return grad_q, key_grads[0], key_grads[1], query_grad, loss[0, 0]


def solution(mesh):
    return jax.shard_map(
        on_device,
        mesh=mesh,
        in_specs=(
            P("seq", "dp", "tensor"),
            P("seq", "dp", "tensor"),
            P("seq", "dp", "tensor"),
            P("seq", "dp", "tensor"),
            P("dp", "tensor"),
            P("dp"),
            P("dp"),
            P("dp", None),
        ),
        out_specs=(
            P("seq", "dp", "tensor"),
            P("seq", "dp", "tensor"),
            P("seq", "dp", "tensor"),
            P("dp", "tensor"),
            P(),
        ),
        check_vma=False,
    )
```

```python
import functools
import math

import jax
import jax.numpy as jnp
from jax import lax
from jax.experimental import pallas as pl
from jax.experimental.pallas import tpu as pltpu
from jax.sharding import PartitionSpec as P

QH = 32
KVH = 8
HD = 128
TAU = 0.02
HARD_BOOST = 3.0
EPS = 1e-06
NEG_BIG = -1e30
SEQ = 16
DP = 4
GROUP = QH // KVH
MESH = pl.DeviceIdType.MESH
NT = (((1,), (1,)), ((), ()))
NN = (((1,), (0,)), ((), ()))
F32 = jnp.float32
BF16 = jnp.bfloat16


def places():
    seq, dp, tensor = lax.axis_index("seq"), lax.axis_index("dp"), lax.axis_index("tensor")
    return seq, dp, tensor, seq // 8, lax.rem(seq // 4, 2), lax.rem(seq, 4)


def remote(src, dst, send, recv, **device):
    return pltpu.make_async_remote_copy(
        src_ref=src, dst_ref=dst, send_sem=send, recv_sem=recv, device_id=device, device_id_type=MESH
    )


def worker(tensor, j):
    return (j // 8) * 8 + tensor * 4 + lax.rem(j // 2, 4), lax.rem(j, 2)


def greet(send_to, count):
    barrier = pltpu.get_barrier_semaphore()
    send_to(lambda **device: pl.semaphore_signal(barrier, inc=1, device_id=device, device_id_type=MESH))
    pl.semaphore_wait(barrier, count)


def when_else(cond, yes, no):
    pl.when(cond)(yes)
    pl.when(jnp.logical_not(cond))(no)


def start_to_workers(src_of, dst_of, send, recv, first=0, end=8):
    seq, _, tensor, _, _, _ = places()

    def body(n, _):
        head = lax.rem(seq + 2 + n, 4)
        doc = lax.rem(seq // 8 + 1 + n // 4, 2)
        for core in range(2):
            j = doc * 8 + head * 2 + core
            peer, _ = worker(tensor, j)
            src, dst = src_of(j, core), dst_of(core)
            when_else(
                (peer == seq) & (core == tensor),
                lambda: pltpu.make_async_copy(src, dst.at[seq], recv.at[seq]).start(),
                lambda: remote(src, dst.at[seq], send.at[j], recv.at[seq], seq=peer, tensor=core).start(),
            )
        return 0

    lax.fori_loop(first, end, body, 0)


def sent_to_workers(src_of, dst_of, send, recv):
    seq, _, tensor, _, _, _ = places()

    def body(n, _):
        for core in range(2):
            j = 2 * n + core
            peer, _ = worker(tensor, j)
            src, dst = src_of(j, core), dst_of(core)
            pl.when(jnp.logical_not((peer == seq) & (core == tensor)))(
                lambda: remote(src, dst.at[seq], send.at[j], recv.at[seq], seq=peer, tensor=core).wait_send()
            )
        return 0

    lax.fori_loop(0, 8, body, 0)


def from_sources(src_of, dst_of, send, recv):
    seq, _, tensor, _, item_tensor, _ = places()
    src, dst = src_of(0, 0), dst_of(tensor)

    def body(s, _):
        when_else(
            (s == seq) & (item_tensor == tensor),
            lambda: pltpu.make_async_copy(src, dst.at[s], recv.at[s]).wait(),
            lambda: remote(src, dst.at[s], send.at[0], recv.at[s], seq=s, tensor=item_tensor).wait_recv(),
        )
        return 0

    lax.fori_loop(0, 16, body, 0)


def to_source(s, src, dst, send, recv, what):
    seq, _, tensor, item_doc, item_tensor, item_head = places()
    slot = item_doc * 8 + item_head * 2 + tensor
    own = (s == seq) & (item_tensor == tensor)
    copy = lambda: remote(src, dst.at[slot], send.at[s], recv.at[slot], seq=s, tensor=item_tensor)
    if what == "start":
        when_else(
            own,
            lambda: pltpu.make_async_copy(src, dst.at[slot], recv.at[slot]).start(),
            lambda: copy().start(),
        )
    else:
        pl.when(jnp.logical_not(own))(lambda: copy().wait_send())


def from_workers(src, dst, send, recv):
    seq, _, tensor, _, _, _ = places()

    def body(j, _):
        peer, core = worker(tensor, j)
        when_else(
            (peer == seq) & (core == tensor),
            lambda: pltpu.make_async_copy(src, dst.at[j], recv.at[j]).wait(),
            lambda: remote(src, dst.at[j], send.at[0], recv.at[j], seq=peer, tensor=core).wait_recv(),
        )
        return 0

    lax.fori_loop(0, 16, body, 0)


def around(buf, send, recv, axis, size, step, src=None):
    me = lax.axis_index(axis)

    def copy(i):
        peer = lax.rem(me + i, size)
        from_ref = buf.at[me] if src is None else src.at[peer]
        return peer, from_ref

    def start(i, _):
        peer, from_ref = copy(i)
        remote(from_ref, buf.at[me], send.at[i], recv.at[me], **{axis: peer}).start()
        return 0

    def finish(i, _):
        peer, from_ref = copy(i)
        remote(from_ref, buf.at[peer], send.at[i], recv.at[peer], **{axis: peer}).wait()
        return 0

    lax.fori_loop(1, size, start if step == "start" else finish, 0)


def fold(x, op):
    return functools.reduce(op, [x[:, j * 128 : (j + 1) * 128] for j in range(x.shape[1] // 128)])


def column_of(row_values, rows):
    at = lax.broadcasted_iota(jnp.int32, (rows, 128), 0) == lax.broadcasted_iota(jnp.int32, (rows, 128), 1)
    return jnp.sum(jnp.where(at, row_values, 0.0), 1, keepdims=True)


def row_of(column):
    rows = column.shape[0]
    at = lax.broadcasted_iota(jnp.int32, (rows, 128), 0) == lax.broadcasted_iota(jnp.int32, (rows, 128), 1)
    return jnp.sum(jnp.where(at, column, 0.0), 0, keepdims=True)


def kernel(
    blk, len_ref, qi, gi, ki, vi, qe_ref, ids_ref,
    dq_out, dkv_out, qgrad_ref, loss_ref,
    q_all, g_all, kv_all, last_buf, part_buf, doc_buf, doc_all, logit_send, logit_recv, grad_send, grad_buf, ql,
    pg_own, pg_peer, s_ref, e_ref, d_ref, kt_ref, vt_ref, mx_ref, l_ref, t_ref, inv_ref, acc_ref, dq_s, keep, other, came, dkv_s,
    qs, qr, gs, gr, ks, kr, as_, ar, bs, br, dqs, dqr, dks, dkr, cs, cr, es, er, xs, xr, ds, dr, fs, fr, ps, pr,
):
    seq, dp, tensor, item_doc, item_tensor, item_head = places()
    rows = qi.shape[1]
    width = qe_ref.shape[1]
    scale = HD ** -0.5
    own_source = (item_tensor == tensor).astype(jnp.int32)

    def greetings(signal):
        def both(j, _):
            pl.when(jnp.logical_not((j == seq) & (item_tensor == tensor)))(lambda: signal(seq=j, tensor=item_tensor))
            peer, core = worker(tensor, j)
            pl.when(jnp.logical_not((peer == seq) & (core == tensor)))(lambda: signal(seq=peer, tensor=core))
            return 0

        lax.fori_loop(0, 16, both, 0)
        lax.fori_loop(1, SEQ, lambda i, c: (signal(seq=lax.rem(seq + i, SEQ)), c)[1], 0)
        lax.fori_loop(1, DP, lambda i, c: (signal(dp=lax.rem(dp + i, DP)), c)[1], 0)
        signal(tensor=1 - tensor)

    greet(greetings, 32 - 2 * own_source + (SEQ - 1) + (DP - 1) + 1)

    q_of, g_of, kv_of = lambda core: q_all, lambda core: g_all, lambda core: kv_all.at[core]
    kv_args = (lambda j, core: (ki, vi)[core].at[j // 2], kv_of, ks, kr)
    q_args = (lambda j, core: qi.at[j], q_of, qs, qr)
    g_args = (lambda j, core: gi.at[j], g_of, gs, gr)

    start = seq * rows
    length = [len_ref[0], len_ref[1]]
    row = lax.broadcasted_iota(jnp.int32, (rows, 1), 0) + start
    for j in range(16):
        at_last = row == length[j // 8] - 1
        picked = jnp.sum(jnp.where(at_last, qi[j].astype(F32), 0.0), 0, keepdims=True)
        ql[2 * j : 2 * j + 1, :] = picked[:, :HD]
        ql[2 * j + 1 : 2 * j + 2, :] = picked[:, HD:]
    last_buf[seq] = ql[...].astype(BF16)
    around(last_buf, as_, ar, "seq", SEQ, "start")
    start_to_workers(*kv_args)
    qf = qe_ref[...].astype(F32)
    query_sq = jnp.sum(qf * qf, -1, keepdims=True)
    around(last_buf, as_, ar, "seq", SEQ, "finish")
    last = functools.reduce(jnp.add, [last_buf[i].astype(F32) for i in range(SEQ)]).astype(BF16)

    head_row = lax.broadcasted_iota(jnp.int32, (32, rows), 0)
    key_pos = lax.broadcasted_iota(jnp.int32, (32, rows), 1) + start
    scores = jnp.zeros((32, rows), F32)
    for j in range(8):
        term = lax.dot_general(last, ki[j], NT, preferred_element_type=F32)
        scores = jnp.where(head_row // GROUP == j, term, scores)
    visible = key_pos < jnp.where(head_row < 16, length[0], length[1])
    scores = jnp.where(visible, scores * scale, NEG_BIG)
    peak = jnp.max(scores, -1, keepdims=True)
    expw = jnp.where(visible, jnp.exp(scores - peak), 0.0)
    total = jnp.sum(expw, -1, keepdims=True)
    weights = expw.astype(BF16)
    mixed = jnp.zeros((32, HD), F32)
    wide_row = lax.broadcasted_iota(jnp.int32, (32, HD), 0)
    for j in range(8):
        term = lax.dot_general(weights, vi[j], NN, preferred_element_type=F32)
        mixed = jnp.where(wide_row // GROUP == j, term, mixed)
    part_buf[seq, :32, :] = mixed
    part_buf[seq, 32:, :] = jnp.zeros((8, 128), F32)
    part_buf[seq, 32:33, :] = row_of(peak)
    part_buf[seq, 33:34, :] = row_of(total)
    around(part_buf, bs, br, "seq", SEQ, "start")
    start_to_workers(*q_args)
    around(part_buf, bs, br, "seq", SEQ, "finish")

    from_sources(*kv_args)
    share = remote(kv_all.at[tensor], kv_all.at[tensor], ps, pr, tensor=1 - tensor)
    share.start()
    peaks = [part_buf[i, 32:33, :] for i in range(SEQ)]
    top = functools.reduce(jnp.maximum, peaks)
    factors = [jnp.exp(p - top) for p in peaks]
    total = functools.reduce(jnp.add, [f * part_buf[i, 33:34, :] for i, f in enumerate(factors)])
    inv_total = 1.0 / jnp.where(total > 0.0, total, 1.0)
    pooled = functools.reduce(jnp.add, [column_of(f * inv_total, 32) * part_buf[i, :32, :] for i, f in enumerate(factors)])
    for d in range(2):
        for h in range(16):
            doc_buf[dp, d : d + 1, h * HD : (h + 1) * HD] = pooled[d * 16 + h : d * 16 + h + 1, :]
    around(doc_buf, cs, cr, "dp", DP, "start")
    start_to_workers(*g_args, 0, 4)
    around(doc_buf, cs, cr, "dp", DP, "finish")
    for i in range(DP):
        doc_all[2 * i : 2 * i + 2, :] = doc_buf[i]

    docs = doc_all[...]
    high = docs.astype(BF16)
    rest = docs - high.astype(F32)
    middle = rest.astype(BF16)
    low = (rest - middle.astype(F32)).astype(BF16)
    terms = jnp.concatenate([low, middle, high, jnp.zeros_like(low)], 0)
    raw = lax.dot_general(qe_ref[...], terms, NT, preferred_element_type=F32)
    raw = raw[:, 0:8] + raw[:, 8:16] + raw[:, 16:24]
    queries = qe_ref.shape[0]
    logit_send[...] = jnp.zeros_like(logit_send)
    logit_send[:queries, 0:8] = raw
    logit_send[:queries, 8:9] = query_sq
    logit_send[queries:, :] = jnp.broadcast_to(jnp.sum(docs * docs, -1, keepdims=True), (8, 128))
    exchange = remote(logit_send, logit_recv, ds, dr, tensor=1 - tensor)
    exchange.start()
    start_to_workers(*g_args, 4, 8)

    share.wait_send()
    remote(kv_all.at[tensor], kv_all.at[1 - tensor], ps, pr, tensor=1 - tensor).wait_recv()
    from_sources(*q_args)
    per = blk // rows
    blocks = SEQ // per
    lines = 2 * blk
    c2 = scale * math.log2(math.e)
    local = lax.rem(lax.broadcasted_iota(jnp.int32, (lines, blk), 0), blk)
    diagonal = local >= lax.broadcasted_iota(jnp.int32, (lines, blk), 1)
    line = lax.rem(lax.broadcasted_iota(jnp.int32, (lines, 1), 0), blk)

    def stacked(ref, i):
        x = ref[pl.ds(i * per, per)].reshape(blk, 2 * HD)
        return jnp.concatenate([x[:, :HD], x[:, HD:]], 0)

    def keys(kind, c):
        return kv_all[kind, pl.ds(c * per, per)].reshape(blk, HD)

    def forward(i, _):
        q = stacked(q_all, i)
        first = i * (i + 1) // 2
        s = lax.dot_general(q, keys(0, i), NT, preferred_element_type=F32)
        s = jnp.where(diagonal, s, NEG_BIG)
        mx_ref[...] = fold(s, jnp.maximum)
        s_ref[i] = s

        def score(c, _):
            s = lax.dot_general(q, keys(0, c), NT, preferred_element_type=F32)
            mx_ref[...] = jnp.maximum(mx_ref[...], fold(s, jnp.maximum))
            s_ref[c] = s
            return 0

        lax.fori_loop(0, i, score, 0)
        m = jnp.max(mx_ref[...], -1, keepdims=True) * c2
        l_ref[...] = jnp.zeros_like(l_ref)

        def weigh(c, _):
            e = jnp.exp2(s_ref[c] * c2 - m)
            l_ref[...] += fold(e, jnp.add)
            e_ref[first + c] = e.astype(BF16)
            return 0

        lax.fori_loop(0, i + 1, weigh, 0)
        inv_ref[i] = jnp.broadcast_to(1.0 / jnp.sum(l_ref[...], -1, keepdims=True), (lines, 128))
        return 0

    lax.fori_loop(0, blocks - 1, forward, 0)
    exchange.wait()
    both = logit_send[...] + logit_recv[...]
    query_norm = jnp.sqrt(both[:queries, 8:9] + EPS)
    doc_norm = jnp.sqrt(both[queries:, :] + EPS)
    norm_row = row_of(doc_norm[:, 0:1])
    ids = lax.broadcasted_iota(jnp.int32, (queries, 128), 1)
    real = ids < 8
    logits = jnp.where(real, both[:queries] / (query_norm * jnp.where(norm_row > 0.0, norm_row, 1.0)) / TAU, 0.0)
    counts = functools.reduce(
        jnp.add, [(ids_ref[:, c : c + 1] == ids).astype(F32) for c in range(1, ids_ref.shape[1])]
    )
    target = (ids_ref[:, 0:1] == ids).astype(F32)
    weighted = jnp.where(real, (1.0 + HARD_BOOST * counts) * jnp.exp(logits), 0.0)
    denom = jnp.sum(weighted, -1, keepdims=True)
    loss_rows = jnp.log(denom) - jnp.sum(target * logits, -1, keepdims=True)
    local_loss = jnp.sum(loss_rows, 0, keepdims=True)
    coef = weighted / denom - target
    inner_row = jnp.sum(coef * logits, 0, keepdims=True)
    doc_unit = docs / doc_norm[:, 0:1]
    by_norm = coef / query_norm
    one_lane = lax.broadcasted_iota(jnp.int32, (1, 128), 1)
    tail = jnp.where(one_lane == 8, local_loss, inner_row)
    for j in range(8):
        term = jnp.sum(by_norm[:, j : j + 1] * qf, 0, keepdims=True) / TAU
        grad_send[j // 2, j % 2 : j % 2 + 1, :width] = term
        grad_send[j // 2, j % 2 : j % 2 + 1, width:] = tail
    around(grad_buf, es, er, "dp", DP, "start", grad_send)
    lax.fori_loop(blocks - 1, blocks, forward, 0)
    qgrad_ref[...] = functools.reduce(jnp.add, [coef[:, j : j + 1] * doc_unit[j : j + 1, :] for j in range(8)]) / TAU
    grad_buf[dp] = grad_send[dp]
    around(grad_buf, es, er, "dp", DP, "finish", grad_send)
    summed = functools.reduce(jnp.add, [grad_buf[i] for i in range(DP)])
    tail = summed[0:1, width:]
    loss = jnp.sum(jnp.where(one_lane == 8, tail, 0.0), -1, keepdims=True) / (queries * DP)
    loss_ref[...] = loss
    own = doc_buf[dp]
    for d in range(2):
        mine = one_lane == 2 * dp + d
        inner = jnp.sum(jnp.where(mine, tail, 0.0), -1, keepdims=True)
        norm = jnp.sum(jnp.where(mine, norm_row, 0.0), -1, keepdims=True)
        pooled_grad = (summed[d : d + 1, :width] - own[d : d + 1, :] / norm * inner) / norm
        for j in range(8):
            pg_own[8 * d + j] = pooled_grad[:, j * 256 : (j + 1) * 256]
    give = remote(pg_own, pg_peer, fs, fr, tensor=1 - tensor)
    give.start()

    give.wait()
    slot = item_doc * 8 + item_head * 2 + tensor
    extra = jnp.where(item_tensor == tensor, pg_own[slot], pg_peer[slot])
    doc_length = jnp.where(item_doc == 0, length[0], length[1])
    half_line = lax.broadcasted_iota(jnp.int32, (lines, 1), 0) < blk
    extra = jnp.where(half_line, extra[:, :HD], extra[:, HD:])
    kt_ref[...] = jnp.zeros_like(kt_ref)
    vt_ref[...] = jnp.zeros_like(vt_ref)
    from_sources(*g_args)

    def send_keys(i, what):
        swap = remote(other.at[i], came.at[i], xs.at[i], xr.at[i], tensor=1 - tensor)
        if what == "finish":
            swap.wait()
            dkv_s[pl.ds(i * per, per)] = (keep[i] + came[i]).astype(BF16).reshape(per, rows, HD)

            def one(p, _):
                s = i * per + p
                to_source(s, dkv_s.at[s], dkv_out, dks, dkr, "start")
                return 0

            lax.fori_loop(0, per, one, 0)
        else:
            swap.start()

    def backward(n, _):
        i = blocks - 1 - n
        first = i * (i + 1) // 2
        q = stacked(q_all, i)
        at = line + i * blk
        g = jnp.where(at < doc_length, stacked(g_all, i).astype(F32), 0.0)
        g = (g + jnp.where(at == doc_length - 1, extra, 0.0)).astype(BF16)
        t_ref[...] = jnp.zeros_like(t_ref)

        def weigh(c, _):
            dp_ = lax.dot_general(g, keys(1, c), NT, preferred_element_type=F32)
            t_ref[...] += fold(e_ref[first + c].astype(F32) * dp_, jnp.add)
            d_ref[c] = dp_.astype(BF16)
            return 0

        lax.fori_loop(0, i + 1, weigh, 0)
        inv = inv_ref[i][:, 0:1]
        d_vec = (jnp.sum(t_ref[...], -1, keepdims=True) * inv).astype(BF16)
        gt = (g.astype(F32) * inv).astype(BF16).T
        qt = (q.astype(F32) * inv).astype(BF16).T
        acc_ref[...] = jnp.zeros_like(acc_ref)

        def spread(c, _):
            ks_ = pl.ds(pl.multiple_of(c * blk, blk), blk)
            e = e_ref[first + c]
            grad_s = e * (d_ref[c] - d_vec)
            vt_ref[:, ks_] += lax.dot_general(gt, e, NN, preferred_element_type=F32)
            kt_ref[:, ks_] += lax.dot_general(qt, grad_s, NN, preferred_element_type=F32)
            acc_ref[...] += lax.dot_general(grad_s, keys(0, c), NN, preferred_element_type=F32)
            return 0

        lax.fori_loop(0, i + 1, spread, 0)
        dq = (acc_ref[...] * (inv * scale)).astype(BF16)
        dq_s[pl.ds(i * per, per)] = jnp.concatenate([dq[:blk], dq[blk:]], 1).reshape(per, rows, 2 * HD)

        def one(p, _):
            s = i * per + p
            to_source(s, dq_s.at[s], dq_out, dqs, dqr, "start")
            return 0

        lax.fori_loop(0, per, one, 0)
        here = pl.ds(pl.multiple_of(i * blk, blk), blk)
        dk = kt_ref[:, here].T * scale
        dv = vt_ref[:, here].T
        keep[i] = jnp.where(tensor == 0, dk, dv)
        other[i] = jnp.where(tensor == 0, dv, dk)
        send_keys(i, "start")
        pl.when(n > 0)(lambda: send_keys(i + 1, "finish"))
        return 0

    lax.fori_loop(0, blocks, backward, 0)
    send_keys(0, "finish")

    from_workers(dq_s.at[0], dq_out, dqs, dqr)
    from_workers(dkv_s.at[0], dkv_out, dks, dkr)

    def sent(s, _):
        to_source(s, dq_s.at[s], dq_out, dqs, dqr, "sent")
        to_source(s, dkv_s.at[s], dkv_out, dks, dkr, "sent")
        return 0

    lax.fori_loop(0, SEQ, sent, 0)
    for args in (kv_args, q_args, g_args):
        sent_to_workers(*args)


def on_device(q_proj, k_proj, v_proj, lm_cotangent, query_emb, doc_lengths, positive_ids, hard_ids):
    rows, docs, half = q_proj.shape
    heads = k_proj.shape[2] // HD
    queries, width = query_emb.shape
    blk = 4 * rows
    blocks, lines = SEQ * rows // blk, 2 * blk
    vmem = pl.BlockSpec(memory_space=pltpu.VMEM)
    smem = pl.BlockSpec(memory_space=pltpu.SMEM)
    dma = pltpu.SemaphoreType.DMA

    def query_parts(x):
        return x.reshape(rows, docs, heads, 2, 2 * HD).transpose(1, 2, 3, 0, 4).reshape(16, rows, 2 * HD)

    def key_parts(x):
        return x.reshape(rows, docs, heads, HD).transpose(1, 2, 0, 3).reshape(8, rows, HD)

    ids = jnp.concatenate((positive_ids[:, None], hard_ids), 1)
    wide, slim = (16, rows, 2 * HD), (16, rows, HD)
    dq, dkv, query_grad, loss = pl.pallas_call(
        functools.partial(kernel, blk),
        name="whole",
        out_shape=[
            jax.ShapeDtypeStruct(wide, BF16),
            jax.ShapeDtypeStruct(slim, BF16),
            jax.ShapeDtypeStruct((queries, width), F32),
            jax.ShapeDtypeStruct((1, 1), F32),
        ],
        in_specs=[smem] + [vmem] * 6,
        out_specs=[vmem] * 4,
        scratch_shapes=[
            pltpu.VMEM(wide, BF16),
            pltpu.VMEM(wide, BF16),
            pltpu.VMEM((2,) + slim, BF16),
            pltpu.VMEM((SEQ, 32, HD), BF16),
            pltpu.VMEM((SEQ, 40, HD), F32),
            pltpu.VMEM((DP, 2, width), F32),
            pltpu.VMEM((8, width), F32),
            pltpu.VMEM((queries + 8, 128), F32),
            pltpu.VMEM((queries + 8, 128), F32),
            pltpu.VMEM((DP, 2, width + 128), F32),
            pltpu.VMEM((DP, 2, width + 128), F32),
            pltpu.VMEM((32, HD), F32),
            pltpu.VMEM((16, 1, 2 * HD), F32),
            pltpu.VMEM((16, 1, 2 * HD), F32),
            pltpu.VMEM((blocks, lines, blk), F32),
            pltpu.VMEM((blocks * (blocks + 1) // 2, lines, blk), BF16),
            pltpu.VMEM((blocks, lines, blk), BF16),
            pltpu.VMEM((HD, blocks * blk), F32),
            pltpu.VMEM((HD, blocks * blk), F32),
            pltpu.VMEM((lines, 128), F32),
            pltpu.VMEM((lines, 128), F32),
            pltpu.VMEM((lines, 128), F32),
            pltpu.VMEM((blocks, lines, 128), F32),
            pltpu.VMEM((lines, 128), F32),
            pltpu.VMEM(wide, BF16),
            pltpu.VMEM((blocks, blk, HD), F32),
            pltpu.VMEM((blocks, blk, HD), F32),
            pltpu.VMEM((blocks, blk, HD), F32),
            pltpu.VMEM(slim, BF16),
        ]
        + [dma((16,))] * 14
        + [dma((DP,))] * 4
        + [dma((blocks,))] * 2
        + [dma] * 6,
        compiler_params=pltpu.CompilerParams(collective_id=0, has_side_effects=True, vmem_limit_bytes=56 * 2**20),
    )(doc_lengths, query_parts(q_proj), query_parts(lm_cotangent), key_parts(k_proj), key_parts(v_proj), query_emb, ids)
    grad_q = dq.reshape(docs, heads * 2, rows, 2 * HD).transpose(2, 0, 1, 3).reshape(rows, docs, half)
    key_grads = dkv.reshape(docs, heads, 2, rows, HD).transpose(2, 3, 0, 1, 4).reshape(2, rows, docs, heads * HD)
    return grad_q, key_grads[0], key_grads[1], query_grad, loss[0, 0]


def solution(mesh):
    return jax.shard_map(
        on_device,
        mesh=mesh,
        in_specs=(
            P("seq", "dp", "tensor"),
            P("seq", "dp", "tensor"),
            P("seq", "dp", "tensor"),
            P("seq", "dp", "tensor"),
            P("dp", "tensor"),
            P("dp"),
            P("dp"),
            P("dp", None),
        ),
        out_specs=(
            P("seq", "dp", "tensor"),
            P("seq", "dp", "tensor"),
            P("seq", "dp", "tensor"),
            P("dp", "tensor"),
            P(),
        ),
        check_vma=False,
    )
```

```python
import functools
import math

import jax
import jax.numpy as jnp
from jax import lax
from jax.experimental import pallas as pl
from jax.experimental.pallas import tpu as pltpu
from jax.sharding import PartitionSpec as P

QH = 32
KVH = 8
HD = 128
TAU = 0.02
HARD_BOOST = 3.0
EPS = 1e-06
NEG_BIG = -1e30
SEQ = 16
DP = 4
GROUP = QH // KVH
MESH = pl.DeviceIdType.MESH
NT = (((1,), (1,)), ((), ()))
NN = (((1,), (0,)), ((), ()))
F32 = jnp.float32
BF16 = jnp.bfloat16


def places():
    seq, dp, tensor = lax.axis_index("seq"), lax.axis_index("dp"), lax.axis_index("tensor")
    return seq, dp, tensor, seq // 8, lax.rem(seq // 4, 2), lax.rem(seq, 4)


def remote(src, dst, send, recv, **device):
    return pltpu.make_async_remote_copy(
        src_ref=src, dst_ref=dst, send_sem=send, recv_sem=recv, device_id=device, device_id_type=MESH
    )


def worker(tensor, j):
    return (j // 8) * 8 + tensor * 4 + lax.rem(j // 2, 4), lax.rem(j, 2)


def greet(send_to, count):
    barrier = pltpu.get_barrier_semaphore()
    send_to(lambda **device: pl.semaphore_signal(barrier, inc=1, device_id=device, device_id_type=MESH))
    pl.semaphore_wait(barrier, count)


def when_else(cond, yes, no):
    pl.when(cond)(yes)
    pl.when(jnp.logical_not(cond))(no)


def turn(n):
    n = lax.rem(n, 4)
    return jnp.where(n == 0, 1, jnp.where(n == 1, 3, jnp.where(n == 2, 2, 0)))


def start_to_workers(src_of, dst_of, send, recv):
    seq, _, tensor, _, _, _ = places()

    def body(core, n, _):
        head = lax.rem(seq + turn(n), 4)
        doc = lax.rem(seq // 8 + n + n // 4, 2)
        j = doc * 8 + head * 2 + core
        peer, _ = worker(tensor, j)
        src, dst = src_of(j, core), dst_of(core)
        when_else(
            (peer == seq) & (core == tensor),
            lambda: pltpu.make_async_copy(src, dst.at[seq], recv.at[seq]).start(),
            lambda: remote(src, dst.at[seq], send.at[j], recv.at[seq], seq=peer, tensor=core).start(),
        )
        return 0

    for core in range(2):
        lax.fori_loop(0, 8, functools.partial(body, core), 0)


def sent_to_workers(src_of, dst_of, send, recv):
    seq, _, tensor, _, _, _ = places()

    def body(n, _):
        for core in range(2):
            j = 2 * n + core
            peer, _ = worker(tensor, j)
            src, dst = src_of(j, core), dst_of(core)
            pl.when(jnp.logical_not((peer == seq) & (core == tensor)))(
                lambda: remote(src, dst.at[seq], send.at[j], recv.at[seq], seq=peer, tensor=core).wait_send()
            )
        return 0

    lax.fori_loop(0, 8, body, 0)


def from_sources(src_of, dst_of, send, recv):
    seq, _, tensor, _, item_tensor, _ = places()
    src, dst = src_of(0, 0), dst_of(tensor)

    def body(s, _):
        when_else(
            (s == seq) & (item_tensor == tensor),
            lambda: pltpu.make_async_copy(src, dst.at[s], recv.at[s]).wait(),
            lambda: remote(src, dst.at[s], send.at[0], recv.at[s], seq=s, tensor=item_tensor).wait_recv(),
        )
        return 0

    lax.fori_loop(0, 16, body, 0)


def to_source(s, src, dst, send, recv, what):
    seq, _, tensor, item_doc, item_tensor, item_head = places()
    slot = item_doc * 8 + item_head * 2 + tensor
    own = (s == seq) & (item_tensor == tensor)
    copy = lambda: remote(src, dst.at[slot], send.at[s], recv.at[slot], seq=s, tensor=item_tensor)
    if what == "start":
        when_else(
            own,
            lambda: pltpu.make_async_copy(src, dst.at[slot], recv.at[slot]).start(),
            lambda: copy().start(),
        )
    else:
        pl.when(jnp.logical_not(own))(lambda: copy().wait_send())


def from_workers(src, dst, send, recv):
    seq, _, tensor, _, _, _ = places()

    def body(j, _):
        peer, core = worker(tensor, j)
        when_else(
            (peer == seq) & (core == tensor),
            lambda: pltpu.make_async_copy(src, dst.at[j], recv.at[j]).wait(),
            lambda: remote(src, dst.at[j], send.at[0], recv.at[j], seq=peer, tensor=core).wait_recv(),
        )
        return 0

    lax.fori_loop(0, 16, body, 0)


def around(buf, send, recv, axis, size, step, src=None):
    me = lax.axis_index(axis)

    def copy(i):
        peer = lax.rem(me + i, size)
        from_ref = buf.at[me] if src is None else src.at[peer]
        return peer, from_ref

    def start(i, _):
        peer, from_ref = copy(i)
        remote(from_ref, buf.at[me], send.at[i], recv.at[me], **{axis: peer}).start()
        return 0

    def finish(i, _):
        peer, from_ref = copy(i)
        remote(from_ref, buf.at[peer], send.at[i], recv.at[peer], **{axis: peer}).wait()
        return 0

    lax.fori_loop(1, size, start if step == "start" else finish, 0)


def fold(x, op):
    return functools.reduce(op, [x[:, j * 128 : (j + 1) * 128] for j in range(x.shape[1] // 128)])


def column_of(row_values, rows):
    at = lax.broadcasted_iota(jnp.int32, (rows, 128), 0) == lax.broadcasted_iota(jnp.int32, (rows, 128), 1)
    return jnp.sum(jnp.where(at, row_values, 0.0), 1, keepdims=True)


def row_of(column):
    rows = column.shape[0]
    at = lax.broadcasted_iota(jnp.int32, (rows, 128), 0) == lax.broadcasted_iota(jnp.int32, (rows, 128), 1)
    return jnp.sum(jnp.where(at, column, 0.0), 0, keepdims=True)


def kernel(
    blk, len_ref, qi, gi, ki, vi, qe_ref, ids_ref,
    dq_out, dkv_out, qgrad_ref, loss_ref,
    q_all, g_all, kv_all, last_buf, part_buf, doc_buf, doc_all, logit_send, logit_recv, grad_send, grad_buf, ql,
    pg_own, pg_peer, s_ref, e_ref, d_ref, kt_ref, vt_ref, mx_ref, l_ref, t_ref, inv_ref, acc_ref, dq_s, keep, other, came, dkv_s,
    qs, qr, gs, gr, ks, kr, as_, ar, bs, br, dqs, dqr, dks, dkr, cs, cr, es, er, xs, xr, ds, dr, fs, fr, ps, pr,
):
    seq, dp, tensor, item_doc, item_tensor, item_head = places()
    rows = qi.shape[1]
    width = qe_ref.shape[1]
    scale = HD ** -0.5
    own_source = (item_tensor == tensor).astype(jnp.int32)

    def greetings(signal):
        def both(j, _):
            pl.when(jnp.logical_not((j == seq) & (item_tensor == tensor)))(lambda: signal(seq=j, tensor=item_tensor))
            peer, core = worker(tensor, j)
            pl.when(jnp.logical_not((peer == seq) & (core == tensor)))(lambda: signal(seq=peer, tensor=core))
            return 0

        lax.fori_loop(0, 16, both, 0)
        lax.fori_loop(1, SEQ, lambda i, c: (signal(seq=lax.rem(seq + i, SEQ)), c)[1], 0)
        lax.fori_loop(1, DP, lambda i, c: (signal(dp=lax.rem(dp + i, DP)), c)[1], 0)
        signal(tensor=1 - tensor)

    greet(greetings, 32 - 2 * own_source + (SEQ - 1) + (DP - 1) + 1)

    q_of, g_of, kv_of = lambda core: q_all, lambda core: g_all, lambda core: kv_all.at[core]
    kv_args = (lambda j, core: (ki, vi)[core].at[j // 2], kv_of, ks, kr)
    q_args = (lambda j, core: qi.at[j], q_of, qs, qr)
    g_args = (lambda j, core: gi.at[j], g_of, gs, gr)

    start = seq * rows
    length = [len_ref[0], len_ref[1]]
    row = lax.broadcasted_iota(jnp.int32, (rows, 1), 0) + start
    for j in range(16):
        at_last = row == length[j // 8] - 1
        picked = jnp.sum(jnp.where(at_last, qi[j].astype(F32), 0.0), 0, keepdims=True)
        ql[2 * j : 2 * j + 1, :] = picked[:, :HD]
        ql[2 * j + 1 : 2 * j + 2, :] = picked[:, HD:]
    last_buf[seq] = ql[...].astype(BF16)
    around(last_buf, as_, ar, "seq", SEQ, "start")
    start_to_workers(*kv_args)
    qf = qe_ref[...].astype(F32)
    query_sq = jnp.sum(qf * qf, -1, keepdims=True)
    around(last_buf, as_, ar, "seq", SEQ, "finish")
    last = functools.reduce(jnp.add, [last_buf[i].astype(F32) for i in range(SEQ)]).astype(BF16)

    head_row = lax.broadcasted_iota(jnp.int32, (32, rows), 0)
    key_pos = lax.broadcasted_iota(jnp.int32, (32, rows), 1) + start
    scores = jnp.zeros((32, rows), F32)
    for j in range(8):
        term = lax.dot_general(last, ki[j], NT, preferred_element_type=F32)
        scores = jnp.where(head_row // GROUP == j, term, scores)
    visible = key_pos < jnp.where(head_row < 16, length[0], length[1])
    scores = jnp.where(visible, scores * scale, NEG_BIG)
    peak = jnp.max(scores, -1, keepdims=True)
    expw = jnp.where(visible, jnp.exp(scores - peak), 0.0)
    total = jnp.sum(expw, -1, keepdims=True)
    weights = expw.astype(BF16)
    mixed = jnp.zeros((32, HD), F32)
    wide_row = lax.broadcasted_iota(jnp.int32, (32, HD), 0)
    for j in range(8):
        term = lax.dot_general(weights, vi[j], NN, preferred_element_type=F32)
        mixed = jnp.where(wide_row // GROUP == j, term, mixed)
    part_buf[seq, :32, :] = mixed
    part_buf[seq, 32:, :] = jnp.zeros((8, 128), F32)
    part_buf[seq, 32:33, :] = row_of(peak)
    part_buf[seq, 33:34, :] = row_of(total)
    around(part_buf, bs, br, "seq", SEQ, "start")
    start_to_workers(*q_args)
    around(part_buf, bs, br, "seq", SEQ, "finish")

    from_sources(*kv_args)
    share = remote(kv_all.at[tensor], kv_all.at[tensor], ps, pr, tensor=1 - tensor)
    share.start()
    peaks = [part_buf[i, 32:33, :] for i in range(SEQ)]
    top = functools.reduce(jnp.maximum, peaks)
    factors = [jnp.exp(p - top) for p in peaks]
    total = functools.reduce(jnp.add, [f * part_buf[i, 33:34, :] for i, f in enumerate(factors)])
    inv_total = 1.0 / jnp.where(total > 0.0, total, 1.0)
    pooled = functools.reduce(jnp.add, [column_of(f * inv_total, 32) * part_buf[i, :32, :] for i, f in enumerate(factors)])
    for d in range(2):
        for h in range(16):
            doc_buf[dp, d : d + 1, h * HD : (h + 1) * HD] = pooled[d * 16 + h : d * 16 + h + 1, :]
    around(doc_buf, cs, cr, "dp", DP, "start")
    around(doc_buf, cs, cr, "dp", DP, "finish")
    for i in range(DP):
        doc_all[2 * i : 2 * i + 2, :] = doc_buf[i]

    docs = doc_all[...]
    high = docs.astype(BF16)
    rest = docs - high.astype(F32)
    middle = rest.astype(BF16)
    low = (rest - middle.astype(F32)).astype(BF16)
    terms = jnp.concatenate([low, middle, high, jnp.zeros_like(low)], 0)
    raw = lax.dot_general(qe_ref[...], terms, NT, preferred_element_type=F32)
    raw = raw[:, 0:8] + raw[:, 8:16] + raw[:, 16:24]
    queries = qe_ref.shape[0]
    logit_send[...] = jnp.zeros_like(logit_send)
    logit_send[:queries, 0:8] = raw
    logit_send[:queries, 8:9] = query_sq
    logit_send[queries:, :] = jnp.broadcast_to(jnp.sum(docs * docs, -1, keepdims=True), (8, 128))
    exchange = remote(logit_send, logit_recv, ds, dr, tensor=1 - tensor)
    exchange.start()
    exchange.wait()
    both = logit_send[...] + logit_recv[...]
    query_norm = jnp.sqrt(both[:queries, 8:9] + EPS)
    doc_norm = jnp.sqrt(both[queries:, :] + EPS)
    norm_row = row_of(doc_norm[:, 0:1])
    ids = lax.broadcasted_iota(jnp.int32, (queries, 128), 1)
    real = ids < 8
    logits = jnp.where(real, both[:queries] / (query_norm * jnp.where(norm_row > 0.0, norm_row, 1.0)) / TAU, 0.0)
    counts = functools.reduce(
        jnp.add, [(ids_ref[:, c : c + 1] == ids).astype(F32) for c in range(1, ids_ref.shape[1])]
    )
    target = (ids_ref[:, 0:1] == ids).astype(F32)
    weighted = jnp.where(real, (1.0 + HARD_BOOST * counts) * jnp.exp(logits), 0.0)
    denom = jnp.sum(weighted, -1, keepdims=True)
    loss_rows = jnp.log(denom) - jnp.sum(target * logits, -1, keepdims=True)
    local_loss = jnp.sum(loss_rows, 0, keepdims=True)
    coef = weighted / denom - target
    inner_row = jnp.sum(coef * logits, 0, keepdims=True)
    doc_unit = docs / doc_norm[:, 0:1]
    by_norm = coef / query_norm
    one_lane = lax.broadcasted_iota(jnp.int32, (1, 128), 1)
    tail = jnp.where(one_lane == 8, local_loss, inner_row)
    for j in range(8):
        term = jnp.sum(by_norm[:, j : j + 1] * qf, 0, keepdims=True) / TAU
        grad_send[j // 2, j % 2 : j % 2 + 1, :width] = term
        grad_send[j // 2, j % 2 : j % 2 + 1, width:] = tail
    around(grad_buf, es, er, "dp", DP, "start", grad_send)
    share.wait_send()
    remote(kv_all.at[tensor], kv_all.at[1 - tensor], ps, pr, tensor=1 - tensor).wait_recv()
    from_sources(*q_args)
    start_to_workers(*g_args)
    per = blk // rows
    blocks = SEQ // per
    lines = 2 * blk
    c2 = scale * math.log2(math.e)
    local = lax.rem(lax.broadcasted_iota(jnp.int32, (lines, blk), 0), blk)
    diagonal = local >= lax.broadcasted_iota(jnp.int32, (lines, blk), 1)
    line = lax.rem(lax.broadcasted_iota(jnp.int32, (lines, 1), 0), blk)

    def stacked(ref, i):
        x = ref[pl.ds(i * per, per)].reshape(blk, 2 * HD)
        return jnp.concatenate([x[:, :HD], x[:, HD:]], 0)

    def keys(kind, c):
        return kv_all[kind, pl.ds(c * per, per)].reshape(blk, HD)

    def forward(i, _):
        q = stacked(q_all, i)
        first = i * (i + 1) // 2
        s = lax.dot_general(q, keys(0, i), NT, preferred_element_type=F32)
        s = jnp.where(diagonal, s, NEG_BIG)
        mx_ref[...] = fold(s, jnp.maximum)
        s_ref[i] = s

        def score(c, _):
            s = lax.dot_general(q, keys(0, c), NT, preferred_element_type=F32)
            mx_ref[...] = jnp.maximum(mx_ref[...], fold(s, jnp.maximum))
            s_ref[c] = s
            return 0

        lax.fori_loop(0, i, score, 0)
        m = jnp.max(mx_ref[...], -1, keepdims=True) * c2
        l_ref[...] = jnp.zeros_like(l_ref)

        def weigh(c, _):
            e = jnp.exp2(s_ref[c] * c2 - m)
            l_ref[...] += fold(e, jnp.add)
            e_ref[first + c] = e.astype(BF16)
            return 0

        lax.fori_loop(0, i + 1, weigh, 0)
        inv_ref[i] = jnp.broadcast_to(1.0 / jnp.sum(l_ref[...], -1, keepdims=True), (lines, 128))
        return 0

    lax.fori_loop(0, blocks, forward, 0)
    qgrad_ref[...] = functools.reduce(jnp.add, [coef[:, j : j + 1] * doc_unit[j : j + 1, :] for j in range(8)]) / TAU
    grad_buf[dp] = grad_send[dp]
    around(grad_buf, es, er, "dp", DP, "finish", grad_send)
    summed = functools.reduce(jnp.add, [grad_buf[i] for i in range(DP)])
    tail = summed[0:1, width:]
    loss = jnp.sum(jnp.where(one_lane == 8, tail, 0.0), -1, keepdims=True) / (queries * DP)
    loss_ref[...] = loss
    own = doc_buf[dp]
    for d in range(2):
        mine = one_lane == 2 * dp + d
        inner = jnp.sum(jnp.where(mine, tail, 0.0), -1, keepdims=True)
        norm = jnp.sum(jnp.where(mine, norm_row, 0.0), -1, keepdims=True)
        pooled_grad = (summed[d : d + 1, :width] - own[d : d + 1, :] / norm * inner) / norm
        for j in range(8):
            pg_own[8 * d + j] = pooled_grad[:, j * 256 : (j + 1) * 256]
    give = remote(pg_own, pg_peer, fs, fr, tensor=1 - tensor)
    give.start()

    give.wait()
    slot = item_doc * 8 + item_head * 2 + tensor
    extra = jnp.where(item_tensor == tensor, pg_own[slot], pg_peer[slot])
    doc_length = jnp.where(item_doc == 0, length[0], length[1])
    half_line = lax.broadcasted_iota(jnp.int32, (lines, 1), 0) < blk
    extra = jnp.where(half_line, extra[:, :HD], extra[:, HD:])
    kt_ref[...] = jnp.zeros_like(kt_ref)
    vt_ref[...] = jnp.zeros_like(vt_ref)
    from_sources(*g_args)

    def backward(n, _):
        i = lax.rem(item_head + n, blocks)
        first = i * (i + 1) // 2
        q = stacked(q_all, i)
        at = line + i * blk
        g = jnp.where(at < doc_length, stacked(g_all, i).astype(F32), 0.0)
        g = (g + jnp.where(at == doc_length - 1, extra, 0.0)).astype(BF16)
        t_ref[...] = jnp.zeros_like(t_ref)

        def weigh(c, _):
            dp_ = lax.dot_general(g, keys(1, c), NT, preferred_element_type=F32)
            t_ref[...] += fold(e_ref[first + c].astype(F32) * dp_, jnp.add)
            d_ref[c] = dp_.astype(BF16)
            return 0

        lax.fori_loop(0, i + 1, weigh, 0)
        inv = inv_ref[i][:, 0:1]
        d_vec = (jnp.sum(t_ref[...], -1, keepdims=True) * inv).astype(BF16)
        gt = (g.astype(F32) * inv).astype(BF16).T
        qt = (q.astype(F32) * inv).astype(BF16).T
        acc_ref[...] = jnp.zeros_like(acc_ref)

        def spread(c, _):
            ks_ = pl.ds(pl.multiple_of(c * blk, blk), blk)
            e = e_ref[first + c]
            grad_s = e * (d_ref[c] - d_vec)
            vt_ref[:, ks_] += lax.dot_general(gt, e, NN, preferred_element_type=F32)
            kt_ref[:, ks_] += lax.dot_general(qt, grad_s, NN, preferred_element_type=F32)
            acc_ref[...] += lax.dot_general(grad_s, keys(0, c), NN, preferred_element_type=F32)
            return 0

        lax.fori_loop(0, i + 1, spread, 0)
        dq = (acc_ref[...] * (inv * scale)).astype(BF16)
        dq_s[pl.ds(i * per, per)] = jnp.concatenate([dq[:blk], dq[blk:]], 1).reshape(per, rows, 2 * HD)

        def one(p, _):
            s = i * per + lax.rem(seq + turn(p), per)
            to_source(s, dq_s.at[s], dq_out, dqs, dqr, "start")
            return 0

        lax.fori_loop(0, per, one, 0)
        return 0

    lax.fori_loop(0, blocks, backward, 0)

    def swap(i):
        return remote(other.at[i], came.at[i], xs.at[i], xr.at[i], tensor=1 - tensor)

    def give_keys(n, _):
        i = lax.rem(item_head + n, blocks)
        here = pl.ds(pl.multiple_of(i * blk, blk), blk)
        dk = kt_ref[:, here].T * scale
        dv = vt_ref[:, here].T
        keep[i] = jnp.where(tensor == 0, dk, dv)
        other[i] = jnp.where(tensor == 0, dv, dk)
        swap(i).start()
        return 0

    def send_keys(n, _):
        i = lax.rem(item_head + n, blocks)
        swap(i).wait()
        dkv_s[pl.ds(i * per, per)] = (keep[i] + came[i]).astype(BF16).reshape(per, rows, HD)

        def one(p, _):
            s = i * per + lax.rem(seq + turn(p), per)
            to_source(s, dkv_s.at[s], dkv_out, dks, dkr, "start")
            return 0

        lax.fori_loop(0, per, one, 0)
        return 0

    lax.fori_loop(0, blocks, give_keys, 0)
    lax.fori_loop(0, blocks, send_keys, 0)

    from_workers(dq_s.at[0], dq_out, dqs, dqr)
    from_workers(dkv_s.at[0], dkv_out, dks, dkr)

    def sent(s, _):
        to_source(s, dq_s.at[s], dq_out, dqs, dqr, "sent")
        to_source(s, dkv_s.at[s], dkv_out, dks, dkr, "sent")
        return 0

    lax.fori_loop(0, SEQ, sent, 0)
    for args in (kv_args, q_args, g_args):
        sent_to_workers(*args)


def on_device(q_proj, k_proj, v_proj, lm_cotangent, query_emb, doc_lengths, positive_ids, hard_ids):
    rows, docs, half = q_proj.shape
    heads = k_proj.shape[2] // HD
    queries, width = query_emb.shape
    blk = 4 * rows
    blocks, lines = SEQ * rows // blk, 2 * blk
    vmem = pl.BlockSpec(memory_space=pltpu.VMEM)
    smem = pl.BlockSpec(memory_space=pltpu.SMEM)
    dma = pltpu.SemaphoreType.DMA

    def query_parts(x):
        return x.reshape(rows, docs, heads, 2, 2 * HD).transpose(1, 2, 3, 0, 4).reshape(16, rows, 2 * HD)

    def key_parts(x):
        return x.reshape(rows, docs, heads, HD).transpose(1, 2, 0, 3).reshape(8, rows, HD)

    ids = jnp.concatenate((positive_ids[:, None], hard_ids), 1)
    wide, slim = (16, rows, 2 * HD), (16, rows, HD)
    dq, dkv, query_grad, loss = pl.pallas_call(
        functools.partial(kernel, blk),
        name="whole",
        out_shape=[
            jax.ShapeDtypeStruct(wide, BF16),
            jax.ShapeDtypeStruct(slim, BF16),
            jax.ShapeDtypeStruct((queries, width), F32),
            jax.ShapeDtypeStruct((1, 1), F32),
        ],
        in_specs=[smem] + [vmem] * 6,
        out_specs=[vmem] * 4,
        scratch_shapes=[
            pltpu.VMEM(wide, BF16),
            pltpu.VMEM(wide, BF16),
            pltpu.VMEM((2,) + slim, BF16),
            pltpu.VMEM((SEQ, 32, HD), BF16),
            pltpu.VMEM((SEQ, 40, HD), F32),
            pltpu.VMEM((DP, 2, width), F32),
            pltpu.VMEM((8, width), F32),
            pltpu.VMEM((queries + 8, 128), F32),
            pltpu.VMEM((queries + 8, 128), F32),
            pltpu.VMEM((DP, 2, width + 128), F32),
            pltpu.VMEM((DP, 2, width + 128), F32),
            pltpu.VMEM((32, HD), F32),
            pltpu.VMEM((16, 1, 2 * HD), F32),
            pltpu.VMEM((16, 1, 2 * HD), F32),
            pltpu.VMEM((blocks, lines, blk), F32),
            pltpu.VMEM((blocks * (blocks + 1) // 2, lines, blk), BF16),
            pltpu.VMEM((blocks, lines, blk), BF16),
            pltpu.VMEM((HD, blocks * blk), F32),
            pltpu.VMEM((HD, blocks * blk), F32),
            pltpu.VMEM((lines, 128), F32),
            pltpu.VMEM((lines, 128), F32),
            pltpu.VMEM((lines, 128), F32),
            pltpu.VMEM((blocks, lines, 128), F32),
            pltpu.VMEM((lines, 128), F32),
            pltpu.VMEM(wide, BF16),
            pltpu.VMEM((blocks, blk, HD), F32),
            pltpu.VMEM((blocks, blk, HD), F32),
            pltpu.VMEM((blocks, blk, HD), F32),
            pltpu.VMEM(slim, BF16),
        ]
        + [dma((16,))] * 14
        + [dma((DP,))] * 4
        + [dma((blocks,))] * 2
        + [dma] * 6,
        compiler_params=pltpu.CompilerParams(collective_id=0, has_side_effects=True, vmem_limit_bytes=56 * 2**20),
    )(doc_lengths, query_parts(q_proj), query_parts(lm_cotangent), key_parts(k_proj), key_parts(v_proj), query_emb, ids)
    grad_q = dq.reshape(docs, heads * 2, rows, 2 * HD).transpose(2, 0, 1, 3).reshape(rows, docs, half)
    key_grads = dkv.reshape(docs, heads, 2, rows, HD).transpose(2, 3, 0, 1, 4).reshape(2, rows, docs, heads * HD)
    return grad_q, key_grads[0], key_grads[1], query_grad, loss[0, 0]


def solution(mesh):
    return jax.shard_map(
        on_device,
        mesh=mesh,
        in_specs=(
            P("seq", "dp", "tensor"),
            P("seq", "dp", "tensor"),
            P("seq", "dp", "tensor"),
            P("seq", "dp", "tensor"),
            P("dp", "tensor"),
            P("dp"),
            P("dp"),
            P("dp", None),
        ),
        out_specs=(
            P("seq", "dp", "tensor"),
            P("seq", "dp", "tensor"),
            P("seq", "dp", "tensor"),
            P("dp", "tensor"),
            P(),
        ),
        check_vma=False,
    )
```

```python
import functools
import math

import jax
import jax.numpy as jnp
from jax import lax
from jax.experimental import pallas as pl
from jax.experimental.pallas import tpu as pltpu
from jax.sharding import PartitionSpec as P

QH = 32
KVH = 8
HD = 128
TAU = 0.02
HARD_BOOST = 3.0
EPS = 1e-06
NEG_BIG = -1e30
SEQ = 16
DP = 4
GROUP = QH // KVH
MESH = pl.DeviceIdType.MESH
NT = (((1,), (1,)), ((), ()))
NN = (((1,), (0,)), ((), ()))
F32 = jnp.float32
BF16 = jnp.bfloat16


def places():
    seq, dp, tensor = lax.axis_index("seq"), lax.axis_index("dp"), lax.axis_index("tensor")
    return seq, dp, tensor, seq // 8, lax.rem(seq // 4, 2), lax.rem(seq, 4)


def remote(src, dst, send, recv, **device):
    return pltpu.make_async_remote_copy(
        src_ref=src, dst_ref=dst, send_sem=send, recv_sem=recv, device_id=device, device_id_type=MESH
    )


def worker(tensor, j):
    return (j // 8) * 8 + tensor * 4 + lax.rem(j // 2, 4), lax.rem(j, 2)


def interleaving(rows, back=False):
    a = lax.broadcasted_iota(jnp.int32, (2 * rows, 2 * rows), 0)
    b = lax.broadcasted_iota(jnp.int32, (2 * rows, 2 * rows), 1)
    if back:
        a, b = b, a
    return (b == 2 * lax.rem(a, rows) + a // rows).astype(F32).astype(BF16)


def moved(matrix, x):
    return lax.dot_general(matrix, x, NN, preferred_element_type=F32).astype(BF16)


def when_else(cond, yes, no):
    pl.when(cond)(yes)
    pl.when(jnp.logical_not(cond))(no)


def turn(n):
    n = lax.rem(n, 4)
    return jnp.where(n == 0, 1, jnp.where(n == 1, 3, jnp.where(n == 2, 2, 0)))


def start_to_workers(src_of, dst_of, send, recv):
    seq, _, tensor, _, _, _ = places()

    def body(core, n, _):
        head = lax.rem(seq + turn(n), 4)
        doc = lax.rem(seq // 8 + n + n // 4, 2)
        j = doc * 8 + head * 2 + core
        peer, _ = worker(tensor, j)
        src, dst = src_of(j, core), dst_of(core)
        when_else(
            (peer == seq) & (core == tensor),
            lambda: pltpu.make_async_copy(src, dst.at[seq], recv.at[seq]).start(),
            lambda: remote(src, dst.at[seq], send.at[j], recv.at[seq], seq=peer, tensor=core).start(),
        )
        return 0

    for core in range(2):
        lax.fori_loop(0, 8, functools.partial(body, core), 0)


def sent_to_workers(src_of, dst_of, send, recv):
    seq, _, tensor, _, _, _ = places()

    def body(n, _):
        for core in range(2):
            j = 2 * n + core
            peer, _ = worker(tensor, j)
            src, dst = src_of(j, core), dst_of(core)
            pl.when(jnp.logical_not((peer == seq) & (core == tensor)))(
                lambda: remote(src, dst.at[seq], send.at[j], recv.at[seq], seq=peer, tensor=core).wait_send()
            )
        return 0

    lax.fori_loop(0, 8, body, 0)


def from_sources(src_of, dst_of, send, recv):
    seq, _, tensor, _, item_tensor, _ = places()
    src, dst = src_of(0, 0), dst_of(tensor)

    def body(s, _):
        when_else(
            (s == seq) & (item_tensor == tensor),
            lambda: pltpu.make_async_copy(src, dst.at[s], recv.at[s]).wait(),
            lambda: remote(src, dst.at[s], send.at[0], recv.at[s], seq=s, tensor=item_tensor).wait_recv(),
        )
        return 0

    lax.fori_loop(0, 16, body, 0)


def to_source(s, src, dst, send, recv, what):
    seq, _, tensor, item_doc, item_tensor, item_head = places()
    slot = item_doc * 8 + item_head * 2 + tensor
    own = (s == seq) & (item_tensor == tensor)
    copy = lambda: remote(src, dst.at[slot], send.at[s], recv.at[slot], seq=s, tensor=item_tensor)
    if what == "start":
        when_else(
            own,
            lambda: pltpu.make_async_copy(src, dst.at[slot], recv.at[slot]).start(),
            lambda: copy().start(),
        )
    else:
        pl.when(jnp.logical_not(own))(lambda: copy().wait_send())


def from_workers(src, dst, send, recv):
    seq, _, tensor, _, _, _ = places()

    def body(j, _):
        peer, core = worker(tensor, j)
        when_else(
            (peer == seq) & (core == tensor),
            lambda: pltpu.make_async_copy(src, dst.at[j], recv.at[j]).wait(),
            lambda: remote(src, dst.at[j], send.at[0], recv.at[j], seq=peer, tensor=core).wait_recv(),
        )
        return 0

    lax.fori_loop(0, 16, body, 0)


def around(buf, send, recv, axis, size, step, src=None):
    me = lax.axis_index(axis)

    def copy(i):
        peer = lax.rem(me + i, size)
        from_ref = buf.at[me] if src is None else src.at[peer]
        return peer, from_ref

    def start(i, _):
        peer, from_ref = copy(i)
        remote(from_ref, buf.at[me], send.at[i], recv.at[me], **{axis: peer}).start()
        return 0

    def finish(i, _):
        peer, from_ref = copy(i)
        remote(from_ref, buf.at[peer], send.at[i], recv.at[peer], **{axis: peer}).wait()
        return 0

    lax.fori_loop(1, size, start if step == "start" else finish, 0)


def fold(x, op):
    return functools.reduce(op, [x[:, j * 128 : (j + 1) * 128] for j in range(x.shape[1] // 128)])


def column_of(row_values, rows):
    lanes = row_values.shape[1]
    at = lax.broadcasted_iota(jnp.int32, (rows, lanes), 0) == lax.broadcasted_iota(jnp.int32, (rows, lanes), 1)
    return jnp.sum(jnp.where(at, row_values, 0.0), 1, keepdims=True)


def row_of(column):
    rows = column.shape[0]
    at = lax.broadcasted_iota(jnp.int32, (rows, 128), 0) == lax.broadcasted_iota(jnp.int32, (rows, 128), 1)
    return jnp.sum(jnp.where(at, column, 0.0), 0, keepdims=True)


def kernel(
    blk, len_ref, q_raw, g_raw, k_raw, v_raw, qe_ref, pos_ref, hard_ref,
    grad_q, grad_k, grad_v, qgrad_ref, loss_ref,
    qi, gi, ki, vi, dq_out, dkv_out,
    q_all, g_all, kv_all, last_buf, part_buf, doc_buf, doc_all, logit_send, logit_recv, grad_send, grad_buf, ql,
    pg_own, pg_peer, s_ref, e_ref, d_ref, kt_ref, vt_ref, mx_ref, l_ref, t_ref, inv_ref, acc_ref, dq_s, keep, other, came, dkv_s,
    qs, qr, gs, gr, ks, kr, as_, ar, bs, br, dqs, dqr, dks, dkr, cs, cr, es, er, xs, xr, ds, dr, fs, fr, ps, pr,
):
    seq, dp, tensor, item_doc, item_tensor, item_head = places()
    rows = qi.shape[1]
    width = qe_ref.shape[1]
    scale = HD ** -0.5
    own_source = (item_tensor == tensor).astype(jnp.int32)

    def greetings(signal):
        def both(j, _):
            pl.when(jnp.logical_not((j == seq) & (item_tensor == tensor)))(lambda: signal(seq=j, tensor=item_tensor))
            peer, core = worker(tensor, j)
            pl.when(jnp.logical_not((peer == seq) & (core == tensor)))(lambda: signal(seq=peer, tensor=core))
            return 0

        lax.fori_loop(0, 16, both, 0)
        lax.fori_loop(1, SEQ, lambda i, c: (signal(seq=lax.rem(seq + i, SEQ)), c)[1], 0)
        lax.fori_loop(1, DP, lambda i, c: (signal(dp=lax.rem(dp + i, DP)), c)[1], 0)
        signal(tensor=1 - tensor)

    barrier = pltpu.get_barrier_semaphore()
    greetings(lambda **device: pl.semaphore_signal(barrier, inc=1, device_id=device, device_id_type=MESH))

    apart = interleaving(rows)

    def split(ref, c):
        both = moved(apart, ref[:, :, c * 256 : (c + 1) * 256].reshape(2 * rows, 256))
        return both[:rows], both[rows:]

    for ref, parts in ((k_raw, ki), (v_raw, vi)):
        for c in range(2):
            for d, part in enumerate(split(ref, c)):
                parts[4 * d + 2 * c] = part[:, :HD]
                parts[4 * d + 2 * c + 1] = part[:, HD:]
    for c in range(8):
        qi[c], qi[8 + c] = split(q_raw, c)

    q_of, g_of, kv_of = lambda core: q_all, lambda core: g_all, lambda core: kv_all.at[core]
    kv_args = (lambda j, core: (ki, vi)[core].at[j // 2], kv_of, ks, kr)
    q_args = (lambda j, core: qi.at[j], q_of, qs, qr)
    g_args = (lambda j, core: gi.at[j], g_of, gs, gr)

    start = seq * rows
    length = [len_ref[0], len_ref[1]]
    row = lax.broadcasted_iota(jnp.int32, (rows, 1), 0) + start
    for j in range(16):
        at_last = row == length[j // 8] - 1
        picked = jnp.sum(jnp.where(at_last, qi[j].astype(F32), 0.0), 0, keepdims=True)
        ql[2 * j : 2 * j + 1, :] = picked[:, :HD]
        ql[2 * j + 1 : 2 * j + 2, :] = picked[:, HD:]
    last_buf[seq] = ql[...].astype(BF16)
    pl.semaphore_wait(barrier, 32 - 2 * own_source + (SEQ - 1) + (DP - 1) + 1)
    around(last_buf, as_, ar, "seq", SEQ, "start")
    start_to_workers(*kv_args)
    qf = qe_ref[...].astype(F32)
    query_sq = jnp.sum(qf * qf, -1, keepdims=True)
    around(last_buf, as_, ar, "seq", SEQ, "finish")
    last = functools.reduce(jnp.add, [last_buf[i].astype(F32) for i in range(SEQ)]).astype(BF16)

    head_row = lax.broadcasted_iota(jnp.int32, (32, rows), 0)
    key_pos = lax.broadcasted_iota(jnp.int32, (32, rows), 1) + start
    scores = jnp.zeros((32, rows), F32)
    for j in range(8):
        term = lax.dot_general(last, ki[j], NT, preferred_element_type=F32)
        scores = jnp.where(head_row // GROUP == j, term, scores)
    visible = key_pos < jnp.where(head_row < 16, length[0], length[1])
    scores = jnp.where(visible, scores * scale, NEG_BIG)
    peak = jnp.max(scores, -1, keepdims=True)
    expw = jnp.where(visible, jnp.exp(scores - peak), 0.0)
    total = jnp.sum(expw, -1, keepdims=True)
    weights = expw.astype(BF16)
    mixed = jnp.zeros((32, HD), F32)
    wide_row = lax.broadcasted_iota(jnp.int32, (32, HD), 0)
    for j in range(8):
        term = lax.dot_general(weights, vi[j], NN, preferred_element_type=F32)
        mixed = jnp.where(wide_row // GROUP == j, term, mixed)
    part_buf[seq, :32, :] = mixed
    part_buf[seq, 32:, :] = jnp.zeros((8, 128), F32)
    part_buf[seq, 32:33, :] = row_of(peak)
    part_buf[seq, 33:34, :] = row_of(total)
    around(part_buf, bs, br, "seq", SEQ, "start")
    start_to_workers(*q_args)
    for c in range(8):
        gi[c], gi[8 + c] = split(g_raw, c)
    around(part_buf, bs, br, "seq", SEQ, "finish")

    from_sources(*kv_args)
    share = remote(kv_all.at[tensor], kv_all.at[tensor], ps, pr, tensor=1 - tensor)
    share.start()
    peaks = [part_buf[i, 32:33, :] for i in range(SEQ)]
    top = functools.reduce(jnp.maximum, peaks)
    factors = [jnp.exp(p - top) for p in peaks]
    total = functools.reduce(jnp.add, [f * part_buf[i, 33:34, :] for i, f in enumerate(factors)])
    inv_total = 1.0 / jnp.where(total > 0.0, total, 1.0)
    pooled = functools.reduce(jnp.add, [column_of(f * inv_total, 32) * part_buf[i, :32, :] for i, f in enumerate(factors)])
    for d in range(2):
        for h in range(16):
            doc_buf[dp, d : d + 1, h * HD : (h + 1) * HD] = pooled[d * 16 + h : d * 16 + h + 1, :]
    around(doc_buf, cs, cr, "dp", DP, "start")
    around(doc_buf, cs, cr, "dp", DP, "finish")
    for i in range(DP):
        doc_all[2 * i : 2 * i + 2, :] = doc_buf[i]

    docs = doc_all[...]
    high = docs.astype(BF16)
    rest = docs - high.astype(F32)
    middle = rest.astype(BF16)
    low = (rest - middle.astype(F32)).astype(BF16)
    terms = jnp.concatenate([low, middle, high, jnp.zeros_like(low)], 0)
    raw = lax.dot_general(qe_ref[...], terms, NT, preferred_element_type=F32)
    raw = raw[:, 0:8] + raw[:, 8:16] + raw[:, 16:24]
    queries = qe_ref.shape[0]
    logit_send[...] = jnp.zeros_like(logit_send)
    logit_send[:queries, 0:8] = raw
    logit_send[:queries, 8:9] = query_sq
    logit_send[queries:, :] = jnp.broadcast_to(jnp.sum(docs * docs, -1, keepdims=True), (8, 128))
    exchange = remote(logit_send, logit_recv, ds, dr, tensor=1 - tensor)
    exchange.start()
    exchange.wait()
    both = logit_send[...] + logit_recv[...]
    query_norm = jnp.sqrt(both[:queries, 8:9] + EPS)
    doc_norm = jnp.sqrt(both[queries:, :] + EPS)
    norm_row = row_of(doc_norm[:, 0:1])
    ids = lax.broadcasted_iota(jnp.int32, (queries, 128), 1)
    real = ids < 8
    logits = jnp.where(real, both[:queries] / (query_norm * jnp.where(norm_row > 0.0, norm_row, 1.0)) / TAU, 0.0)
    lane_ids = ids.astype(F32)
    counts = functools.reduce(
        jnp.add,
        [(column_of(hard_ref[c : c + 1, :].astype(F32), queries) == lane_ids).astype(F32) for c in range(hard_ref.shape[0])],
    )
    target = (column_of(pos_ref[...].astype(F32), queries) == lane_ids).astype(F32)
    weighted = jnp.where(real, (1.0 + HARD_BOOST * counts) * jnp.exp(logits), 0.0)
    denom = jnp.sum(weighted, -1, keepdims=True)
    loss_rows = jnp.log(denom) - jnp.sum(target * logits, -1, keepdims=True)
    local_loss = jnp.sum(loss_rows, 0, keepdims=True)
    coef = weighted / denom - target
    inner_row = jnp.sum(coef * logits, 0, keepdims=True)
    doc_unit = docs / doc_norm[:, 0:1]
    by_norm = coef / query_norm
    one_lane = lax.broadcasted_iota(jnp.int32, (1, 128), 1)
    tail = jnp.where(one_lane == 8, local_loss, inner_row)
    for j in range(8):
        term = jnp.sum(by_norm[:, j : j + 1] * qf, 0, keepdims=True) / TAU
        grad_send[j // 2, j % 2 : j % 2 + 1, :width] = term
        grad_send[j // 2, j % 2 : j % 2 + 1, width:] = tail
    around(grad_buf, es, er, "dp", DP, "start", grad_send)
    share.wait_send()
    remote(kv_all.at[tensor], kv_all.at[1 - tensor], ps, pr, tensor=1 - tensor).wait_recv()
    from_sources(*q_args)
    start_to_workers(*g_args)
    per = blk // rows
    blocks = SEQ // per
    lines = 2 * blk
    c2 = scale * math.log2(math.e)
    local = lax.rem(lax.broadcasted_iota(jnp.int32, (lines, blk), 0), blk)
    diagonal = local >= lax.broadcasted_iota(jnp.int32, (lines, blk), 1)
    line = lax.rem(lax.broadcasted_iota(jnp.int32, (lines, 1), 0), blk)

    def stacked(ref, i):
        x = ref[pl.ds(i * per, per)].reshape(blk, 2 * HD)
        return jnp.concatenate([x[:, :HD], x[:, HD:]], 0)

    def keys(kind, c):
        return kv_all[kind, pl.ds(c * per, per)].reshape(blk, HD)

    def forward(i, _):
        q = stacked(q_all, i)
        first = i * (i + 1) // 2
        s = lax.dot_general(q, keys(0, i), NT, preferred_element_type=F32)
        s = jnp.where(diagonal, s, NEG_BIG)
        mx_ref[...] = fold(s, jnp.maximum)
        s_ref[i] = s

        def score(c, _):
            s = lax.dot_general(q, keys(0, c), NT, preferred_element_type=F32)
            mx_ref[...] = jnp.maximum(mx_ref[...], fold(s, jnp.maximum))
            s_ref[c] = s
            return 0

        lax.fori_loop(0, i, score, 0)
        m = jnp.max(mx_ref[...], -1, keepdims=True) * c2
        l_ref[...] = jnp.zeros_like(l_ref)

        def weigh(c, _):
            e = jnp.exp2(s_ref[c] * c2 - m)
            l_ref[...] += fold(e, jnp.add)
            e_ref[first + c] = e.astype(BF16)
            return 0

        lax.fori_loop(0, i + 1, weigh, 0)
        inv_ref[i] = jnp.broadcast_to(1.0 / jnp.sum(l_ref[...], -1, keepdims=True), (lines, 128))
        return 0

    lax.fori_loop(0, blocks, forward, 0)
    qgrad_ref[...] = functools.reduce(jnp.add, [coef[:, j : j + 1] * doc_unit[j : j + 1, :] for j in range(8)]) / TAU
    grad_buf[dp] = grad_send[dp]
    around(grad_buf, es, er, "dp", DP, "finish", grad_send)
    summed = functools.reduce(jnp.add, [grad_buf[i] for i in range(DP)])
    tail = summed[0:1, width:]
    loss = jnp.sum(jnp.where(one_lane == 8, tail, 0.0), -1, keepdims=True) / (queries * DP)
    loss_ref[...] = loss
    own = doc_buf[dp]
    for d in range(2):
        mine = one_lane == 2 * dp + d
        inner = jnp.sum(jnp.where(mine, tail, 0.0), -1, keepdims=True)
        norm = jnp.sum(jnp.where(mine, norm_row, 0.0), -1, keepdims=True)
        pooled_grad = (summed[d : d + 1, :width] - own[d : d + 1, :] / norm * inner) / norm
        for j in range(8):
            pg_own[8 * d + j] = pooled_grad[:, j * 256 : (j + 1) * 256]
    give = remote(pg_own, pg_peer, fs, fr, tensor=1 - tensor)
    give.start()

    give.wait()
    slot = item_doc * 8 + item_head * 2 + tensor
    extra = jnp.where(item_tensor == tensor, pg_own[slot], pg_peer[slot])
    doc_length = jnp.where(item_doc == 0, length[0], length[1])
    half_line = lax.broadcasted_iota(jnp.int32, (lines, 1), 0) < blk
    extra = jnp.where(half_line, extra[:, :HD], extra[:, HD:])
    kt_ref[...] = jnp.zeros_like(kt_ref)
    vt_ref[...] = jnp.zeros_like(vt_ref)
    from_sources(*g_args)

    def backward(n, _):
        i = lax.rem(item_head + n, blocks)
        first = i * (i + 1) // 2
        q = stacked(q_all, i)
        at = line + i * blk
        g = jnp.where(at < doc_length, stacked(g_all, i).astype(F32), 0.0)
        g = (g + jnp.where(at == doc_length - 1, extra, 0.0)).astype(BF16)
        t_ref[...] = jnp.zeros_like(t_ref)

        def weigh(c, _):
            dp_ = lax.dot_general(g, keys(1, c), NT, preferred_element_type=F32)
            t_ref[...] += fold(e_ref[first + c].astype(F32) * dp_, jnp.add)
            d_ref[c] = dp_.astype(BF16)
            return 0

        lax.fori_loop(0, i + 1, weigh, 0)
        inv = inv_ref[i][:, 0:1]
        d_vec = (jnp.sum(t_ref[...], -1, keepdims=True) * inv).astype(BF16)
        gt = (g.astype(F32) * inv).astype(BF16).T
        qt = (q.astype(F32) * inv).astype(BF16).T
        acc_ref[...] = jnp.zeros_like(acc_ref)

        def spread(c, _):
            ks_ = pl.ds(pl.multiple_of(c * blk, blk), blk)
            e = e_ref[first + c]
            grad_s = e * (d_ref[c] - d_vec)
            vt_ref[:, ks_] += lax.dot_general(gt, e, NN, preferred_element_type=F32)
            kt_ref[:, ks_] += lax.dot_general(qt, grad_s, NN, preferred_element_type=F32)
            acc_ref[...] += lax.dot_general(grad_s, keys(0, c), NN, preferred_element_type=F32)
            return 0

        lax.fori_loop(0, i + 1, spread, 0)
        dq = (acc_ref[...] * (inv * scale)).astype(BF16)
        dq_s[pl.ds(i * per, per)] = jnp.concatenate([dq[:blk], dq[blk:]], 1).reshape(per, rows, 2 * HD)

        def one(p, _):
            s = i * per + lax.rem(seq + turn(p), per)
            to_source(s, dq_s.at[s], dq_out, dqs, dqr, "start")
            return 0

        lax.fori_loop(0, per, one, 0)
        return 0

    lax.fori_loop(0, blocks, backward, 0)

    def swap(i):
        return remote(other.at[i], came.at[i], xs.at[i], xr.at[i], tensor=1 - tensor)

    def give_keys(n, _):
        i = lax.rem(item_head + n, blocks)
        here = pl.ds(pl.multiple_of(i * blk, blk), blk)
        dk = kt_ref[:, here].T * scale
        dv = vt_ref[:, here].T
        keep[i] = jnp.where(tensor == 0, dk, dv)
        other[i] = jnp.where(tensor == 0, dv, dk)
        swap(i).start()
        return 0

    def send_keys(n, _):
        i = lax.rem(item_head + n, blocks)
        swap(i).wait()
        dkv_s[pl.ds(i * per, per)] = (keep[i] + came[i]).astype(BF16).reshape(per, rows, HD)

        def one(p, _):
            s = i * per + lax.rem(seq + turn(p), per)
            to_source(s, dkv_s.at[s], dkv_out, dks, dkr, "start")
            return 0

        lax.fori_loop(0, per, one, 0)
        return 0

    lax.fori_loop(0, blocks, give_keys, 0)
    lax.fori_loop(0, blocks, send_keys, 0)

    from_workers(dq_s.at[0], dq_out, dqs, dqr)
    together = interleaving(rows, True)
    for c in range(8):
        both = moved(together, jnp.concatenate([dq_out[c], dq_out[8 + c]], 0))
        grad_q[:, :, c * 256 : (c + 1) * 256] = both.reshape(rows, 2, 256)
    from_workers(dkv_s.at[0], dkv_out, dks, dkr)
    for kind, ref in enumerate((grad_k, grad_v)):
        for c in range(2):
            of_doc = [
                jnp.concatenate([dkv_out[8 * d + 4 * c + kind], dkv_out[8 * d + 4 * c + 2 + kind]], 1) for d in range(2)
            ]
            both = moved(together, jnp.concatenate(of_doc, 0))
            ref[:, :, c * 256 : (c + 1) * 256] = both.reshape(rows, 2, 256)

    def sent(s, _):
        to_source(s, dq_s.at[s], dq_out, dqs, dqr, "sent")
        to_source(s, dkv_s.at[s], dkv_out, dks, dkr, "sent")
        return 0

    lax.fori_loop(0, SEQ, sent, 0)
    for args in (kv_args, q_args, g_args):
        sent_to_workers(*args)


def on_device(q_proj, k_proj, v_proj, lm_cotangent, query_emb, doc_lengths, positive_ids, hard_ids):
    rows, docs, half = q_proj.shape
    queries, width = query_emb.shape
    blk = 4 * rows
    blocks, lines = SEQ * rows // blk, 2 * blk
    vmem = pl.BlockSpec(memory_space=pltpu.VMEM)
    smem = pl.BlockSpec(memory_space=pltpu.SMEM)
    dma = pltpu.SemaphoreType.DMA

    wide, slim = (16, rows, 2 * HD), (16, rows, HD)
    grad_q, grad_k, grad_v, query_grad, loss = pl.pallas_call(
        functools.partial(kernel, blk),
        name="whole",
        out_shape=[
            jax.ShapeDtypeStruct(q_proj.shape, BF16),
            jax.ShapeDtypeStruct(k_proj.shape, BF16),
            jax.ShapeDtypeStruct(v_proj.shape, BF16),
            jax.ShapeDtypeStruct((queries, width), F32),
            jax.ShapeDtypeStruct((1, 1), F32),
        ],
        in_specs=[smem] + [vmem] * 7,
        out_specs=[vmem] * 5,
        scratch_shapes=[
            pltpu.VMEM(wide, BF16),
            pltpu.VMEM(wide, BF16),
            pltpu.VMEM((8, rows, HD), BF16),
            pltpu.VMEM((8, rows, HD), BF16),
            pltpu.VMEM(wide, BF16),
            pltpu.VMEM(slim, BF16),
            pltpu.VMEM(wide, BF16),
            pltpu.VMEM(wide, BF16),
            pltpu.VMEM((2,) + slim, BF16),
            pltpu.VMEM((SEQ, 32, HD), BF16),
            pltpu.VMEM((SEQ, 40, HD), F32),
            pltpu.VMEM((DP, 2, width), F32),
            pltpu.VMEM((8, width), F32),
            pltpu.VMEM((queries + 8, 128), F32),
            pltpu.VMEM((queries + 8, 128), F32),
            pltpu.VMEM((DP, 2, width + 128), F32),
            pltpu.VMEM((DP, 2, width + 128), F32),
            pltpu.VMEM((32, HD), F32),
            pltpu.VMEM((16, 1, 2 * HD), F32),
            pltpu.VMEM((16, 1, 2 * HD), F32),
            pltpu.VMEM((blocks, lines, blk), F32),
            pltpu.VMEM((blocks * (blocks + 1) // 2, lines, blk), BF16),
            pltpu.VMEM((blocks, lines, blk), BF16),
            pltpu.VMEM((HD, blocks * blk), F32),
            pltpu.VMEM((HD, blocks * blk), F32),
            pltpu.VMEM((lines, 128), F32),
            pltpu.VMEM((lines, 128), F32),
            pltpu.VMEM((lines, 128), F32),
            pltpu.VMEM((blocks, lines, 128), F32),
            pltpu.VMEM((lines, 128), F32),
            pltpu.VMEM(wide, BF16),
            pltpu.VMEM((blocks, blk, HD), F32),
            pltpu.VMEM((blocks, blk, HD), F32),
            pltpu.VMEM((blocks, blk, HD), F32),
            pltpu.VMEM(slim, BF16),
        ]
        + [dma((16,))] * 14
        + [dma((DP,))] * 4
        + [dma((blocks,))] * 2
        + [dma] * 6,
        compiler_params=pltpu.CompilerParams(collective_id=0, has_side_effects=True, vmem_limit_bytes=56 * 2**20),
    )(
        doc_lengths, q_proj, lm_cotangent, k_proj, v_proj, query_emb, positive_ids.reshape(1, queries), hard_ids.T
    )
    return grad_q, grad_k, grad_v, query_grad, loss.reshape(())


def solution(mesh):
    return jax.shard_map(
        on_device,
        mesh=mesh,
        in_specs=(
            P("seq", "dp", "tensor"),
            P("seq", "dp", "tensor"),
            P("seq", "dp", "tensor"),
            P("seq", "dp", "tensor"),
            P("dp", "tensor"),
            P("dp"),
            P("dp"),
            P("dp", None),
        ),
        out_specs=(
            P("seq", "dp", "tensor"),
            P("seq", "dp", "tensor"),
            P("seq", "dp", "tensor"),
            P("dp", "tensor"),
            P(),
        ),
        check_vma=False,
    )
```
